256 devices in a mesh: row: 16 (over z, x_hi), col: 16 (over y, x_lo, core).
Axes of the slice: x: 4 (x_hi: 2, x_lo: 2; x = x_hi * 2 + x_lo), y: 4, z: 8, core: 2. Of those that a mesh axis runs over, the one named last changes fastest.
Arguments:
- schur: float32 [16, 16, 1024, 1024], P('row', 'col'), as said below
- load: float32 [16, 16, 1024, 256], P('row', 'col')
- dscale: float32 [16, 16, 1024], P('row', 'col'), may hold values from 0.3 to 3
- basis: float32 [16, 16, 8, 1024], P('row', 'col'), may hold values from -1.2 to 1.2
- coarse_inv: float32 [2048, 2048], P(('row', 'col')), as said below
- north_match: int32 [16, 16, 256], P('row', 'col'), may hold values from 0 to 255, each once within a row
- west_match: int32 [16, 16, 256], P('row', 'col'), may hold values from 0 to 255, each once within a row
Outputs:
- solution: float32 [16, 16, 1024, 256], P('row', 'col')
- residual: float32 [16, 16, 1024, 256], P('row', 'col')
The draws below stay inside these ranges and needn't reach their ends.
Inputs may be any that keep to these rules, and one draw needn't show every extreme that they name: schur is symmetric positive definite for every subdomain. coarse_inv is symmetric positive definite. `north_match`: each row of the last dimension is a permutation of 0 to 255. `west_match`: each row of the last dimension is a permutation of 0 to 255.
All inputs are finite; a program needn't handle non-finite values.
Results may differ from the reference program's by a relative error of at most 0.0003.
Values sent between devices are 32-bit elements; how exact they have to be, the bound alone decides.
A program may use at most 128 MiB of HBM per device.

```python
import math
import jax
import jax.numpy as jnp
from jax import lax

F = 256
NI = 1024
SC = 256
K = 8
ITERS = 3
SROWS = 16
SCOLS = 16
NCOARSE = 2048


def symmetric_draw(key, lead_shape, order, diag_lo, diag_hi):
    key_off, key_diag = jax.random.split(key)
    noise = jax.random.uniform(key_off, lead_shape + (order, order), jnp.float32, -1.0, 1.0)
    sym = (noise + jnp.swapaxes(noise, -1, -2)) * (0.35 * math.sqrt(1.5 / order))
    diag_vals = jnp.exp(jax.random.uniform(key_diag, lead_shape + (order,), jnp.float32, math.log(diag_lo), math.log(diag_hi)))
    row_ids = lax.broadcasted_iota(jnp.int32, (order, order), 0)
    col_ids = lax.broadcasted_iota(jnp.int32, (order, order), 1)
    return jnp.where(row_ids == col_ids, diag_vals[..., None], sym)


def draw_schur(key, part):
    key = jax.random.fold_in(key, 11)
    return symmetric_draw(key, (SROWS, SCOLS), NI, 1.0, 3.0)


def draw_coarse_inv(key, part):
    key = jax.random.fold_in(key, 23)
    return symmetric_draw(key, (), NCOARSE, 1.0, 2.0)


def draw_load(key, part):
    key = jax.random.fold_in(key, 37)
    key_base, key_rows, key_cols = jax.random.split(key, 3)
    shape = (SROWS, SCOLS, NI, SC)
    base = jax.random.truncated_normal(key_base, -5.0, 5.0, shape, jnp.float32)
    row_scale = jnp.exp(jax.random.uniform(key_rows, (SROWS, SCOLS, NI, 1), jnp.float32, 0.0, math.log(10.0)))
    col_scale = jnp.exp(jax.random.uniform(key_cols, (1, 1, 1, SC), jnp.float32, 0.0, math.log(10.0)))
    flat_pos = lax.broadcasted_iota(jnp.float32, (SROWS, SCOLS, 1, 1), 0) * SCOLS + lax.broadcasted_iota(jnp.float32, (SROWS, SCOLS, 1, 1), 1)
    trend = 1.0 + 2.0 * flat_pos / max(SROWS * SCOLS - 1, 1)
    return (0.03 * base * row_scale * col_scale * trend).astype(jnp.float32)


def levels(rng, extent, shards, smallest, largest):
    level, own = 1.0, jax.random.fold_in(rng, 6)
    for axis_at, shards_of in shards:
        steps = jnp.exp(jax.random.uniform(jax.random.fold_in(own, axis_at), (shards_of,), jnp.float32, smallest / len(shards), largest / len(shards)))
        level = level * jnp.repeat(steps, extent[axis_at] // shards_of).reshape([-1 if axis == axis_at else 1 for axis in range(len(extent))])
    return level


def scatter_about(own_key, shape, deviation, most, cuts=(), held_as=jnp.bfloat16):
    values = jax.random.normal(own_key, shape, jnp.float32) * deviation
    if len(cuts) > 0:
        values = levels(own_key, shape, cuts, -0.22, 0.18) * values
    return jnp.clip(values, min=-most, max=most).astype(held_as)


def setup_inputs(seed: int = 0) -> dict:
    splits = jax.random.split(jax.random.key(seed), 8)
    schur = draw_schur(jax.random.fold_in(splits[7], 71), 0)
    load = draw_load(jax.random.fold_in(splits[7], 71), 0)
    dscale = jnp.clip(jnp.exp(math.log(3.0) - 2.3025851 * jax.random.uniform(splits[2], (SROWS, SCOLS, NI), jnp.float32) ** levels(splits[2], (SROWS, SCOLS, NI), ((0, 16), (1, 16)), -0.2, 0.2)), 0.3, 3.0)
    basis = scatter_about(splits[3], (SROWS, SCOLS, K, NI), 0.2, 1.2, ((0, 16), (1, 16)), jnp.float32)
    coarse_inv = draw_coarse_inv(jax.random.fold_in(splits[7], 71), 0)
    north_match = jax.vmap(lambda own: jax.random.permutation(own, F))(jax.random.split(splits[5], SROWS * SCOLS)).reshape((SROWS, SCOLS, F)).astype(jnp.int32)
    west_match = jax.vmap(lambda own: jax.random.permutation(own, F))(jax.random.split(splits[6], SROWS * SCOLS)).reshape((SROWS, SCOLS, F)).astype(jnp.int32)
    return dict(schur=schur, load=load, dscale=dscale, basis=basis, coarse_inv=coarse_inv, north_match=north_match, west_match=west_match)


def face_weights():
    rows = jnp.arange(SROWS)[:, None] + jnp.zeros((1, SCOLS), jnp.int32)
    cols = jnp.arange(SCOLS)[None, :] + jnp.zeros((SROWS, 1), jnp.int32)
    north_wt = jnp.where(rows > 0, 0.5, 1.0)
    south_wt = jnp.where(rows < SROWS - 1, 0.5, 1.0)
    west_wt = jnp.where(cols > 0, 0.5, 1.0)
    east_wt = jnp.where(cols < SCOLS - 1, 0.5, 1.0)
    stacked = jnp.stack([north_wt, south_wt, west_wt, east_wt], axis=2).astype(jnp.float32)
    return stacked[:, :, :, None, None]


def permute_rows(block, order):
    return jnp.take_along_axis(block, order[:, :, :, None].astype(jnp.int32), axis=2)


def place_one(block, order):
    return jnp.zeros_like(block).at[order].set(block)


def place_rows(block, order):
    return jax.vmap(jax.vmap(place_one))(block, order)


def assemble(vec, north_match, west_match):
    north_face, south_face, west_face, east_face = vec[:, :, 0], vec[:, :, 1], vec[:, :, 2], vec[:, :, 3]
    pad_row_top = ((1, 0), (0, 0), (0, 0), (0, 0))
    pad_row_bottom = ((0, 1), (0, 0), (0, 0), (0, 0))
    pad_col_left = ((0, 0), (1, 0), (0, 0), (0, 0))
    pad_col_right = ((0, 0), (0, 1), (0, 0), (0, 0))
    from_above = jnp.pad(south_face[:-1], pad_row_top)
    north_new = north_face + permute_rows(from_above, north_match)
    placed_north = place_rows(north_face, north_match)
    south_new = south_face + jnp.pad(placed_north[1:], pad_row_bottom)
    from_left = jnp.pad(east_face[:, :-1], pad_col_left)
    west_new = west_face + permute_rows(from_left, west_match)
    placed_west = place_rows(west_face, west_match)
    east_new = east_face + jnp.pad(placed_west[:, 1:], pad_col_right)
    return jnp.stack([north_new, south_new, west_new, east_new], axis=2)


def reference(schur, load, dscale, basis, coarse_inv, north_match, west_match):
    highest = lax.Precision.HIGHEST
    weight = face_weights()
    scale_five = dscale.reshape(SROWS, SCOLS, 4, F, 1)

    def inner(left, right):
        return jnp.sum(weight * left * right, axis=(0, 1, 2, 3))

    def operate(vec):
        flat_rows = vec.reshape(SROWS, SCOLS, NI, SC)
        product = jnp.einsum("abij,abjs->abis", schur, flat_rows, precision=highest)
        return assemble(product.reshape(SROWS, SCOLS, 4, F, SC), north_match, west_match)

    def precondition(vec):
        weighted = weight * vec
        flat_rows = weighted.reshape(SROWS, SCOLS, NI, SC)
        coarse = jnp.einsum("abkn,abns->abks", basis, flat_rows, precision=highest)
        solved = jnp.dot(coarse_inv, coarse.reshape(NCOARSE, SC), precision=highest)
        solved = solved.reshape(SROWS, SCOLS, K, SC)
        back = jnp.einsum("abkn,abks->abns", basis, solved, precision=highest)
        local_part = weight * (scale_five * weighted + back.reshape(SROWS, SCOLS, 4, F, SC))
        return assemble(local_part, north_match, west_match)

    residual = assemble(load.reshape(SROWS, SCOLS, 4, F, SC), north_match, west_match)
    solution = jnp.zeros_like(residual)
    pre = precondition(residual)
    direction = pre
    rz_now = inner(residual, pre)
    for iteration in range(ITERS):
        image = operate(direction)
        step_len = rz_now / inner(direction, image)
        solution = solution + step_len * direction
        residual = residual - step_len * image
        if iteration + 1 < ITERS:
            pre = precondition(residual)
            rz_next = inner(residual, pre)
            direction = pre + (rz_next / rz_now) * direction
            rz_now = rz_next
    return solution.reshape(SROWS, SCOLS, NI, SC), residual.reshape(SROWS, SCOLS, NI, SC)
```

```python
import functools

import jax
import jax.numpy as jnp
from jax import lax
from jax.experimental import pallas as pl
from jax.experimental.pallas import tpu as pltpu
from jax.sharding import PartitionSpec as P

MESH = pl.DeviceIdType.MESH
F = 256
NI = 1024
SC = 256
K = 8
N = 16
SB = 16
ROUNDS = 4
CHUNKS = 4
OPP = (1, 0, 3, 2)
f32, bf16 = jnp.float32, jnp.bfloat16
NT = (((1,), (1,)), ((), ()))


def mm(a, b):
    return jnp.dot(a, b, preferred_element_type=f32)


def mm_nt(a, b):
    return lax.dot_general(a, b, NT, preferred_element_type=f32)


def split(x):
    hi = x.astype(bf16)
    return hi, (x - hi.astype(f32)).astype(bf16)


def split3(x):
    hi = x.astype(bf16)
    rest = x - hi.astype(f32)
    mid = rest.astype(bf16)
    return hi, mid, (rest - mid.astype(f32)).astype(bf16)


def kernel(
    schur, load, dscale, basis, cinv, north, west,
    sol_out, res_out,
    smat, shi, slo, y, u, r, p, s, x, uhi, ulo, dcol,
    pn, pw, bds, nbr_bds, bext, bst, gst, bcat, tcat, tau, sig,
    crow, chi, clo,
    halo, p1s, p1r, ns, nr, p2s, p2r, p3s, p3r, ts, tr,
    local_sem, hs, hr, bs, br, cs, cr, s1, r1, s15, r15, s2, r2, s3, r3, s35, r35,
):
    row, col = lax.axis_index("row"), lax.axis_index("col")
    has = (row > 0, row < N - 1, col > 0, col < N - 1)
    nbr = ((row - 1, col), (row + 1, col), (row, col - 1), (row, col + 1))
    wt = [jnp.where(h, 0.5, 1.0).astype(f32) for h in has]

    get_s = pltpu.make_async_copy(schur, smat, local_sem.at[0])
    get_load = pltpu.make_async_copy(load, y, local_sem.at[1])
    get_load.start()
    get_s.start()

    barrier = pltpu.get_barrier_semaphore()

    def greet(i, _):
        pl.semaphore_signal(barrier, inc=1, device_id=(lax.rem(row + i, N), col), device_id_type=MESH)
        pl.semaphore_signal(barrier, inc=1, device_id=(row, lax.rem(col + i, N)), device_id_type=MESH)
        return 0

    lax.fori_loop(1, N, greet, 0)

    slot = lax.broadcasted_iota(jnp.int32, (F, F), 0)
    pn[...] = jnp.where(slot == north[...], 1.0, 0.0).astype(bf16)
    pw[...] = jnp.where(slot == west[...], 1.0, 0.0).astype(bf16)

    for f in range(4):

        @pl.when(jnp.logical_not(has[f]))
        def _():
            nbr_bds[f] = jnp.zeros((16, F), f32)
            for rd in range(ROUNDS):
                halo[rd, f] = jnp.zeros((F, SC), f32)
            if f < 2:
                for rd in range(ROUNDS - 1):
                    nr[rd, f] = jnp.zeros((SB, 128), f32)
                    tr[rd, f] = jnp.zeros((K, SC), f32)

    bds[0:8] = basis[...]
    bds[8:16] = jnp.where(lax.broadcasted_iota(jnp.int32, (8, NI), 0) == 0, dscale[...], 0.0)
    for f, perm in ((0, pn), (2, pw)):
        parts = split3(bds[:, f * F : (f + 1) * F])
        hi, mid, lo = [mm_nt(part, perm[...]) for part in parts]
        bds[:, f * F : (f + 1) * F] = (hi + mid) + lo

    pl.semaphore_wait(barrier, 2 * (N - 1))

    def when_each(fn, faces=(0, 1, 2, 3)):
        for f in faces:
            pl.when(has[f])(functools.partial(fn, f))

    def face_basis(f):
        return pltpu.make_async_remote_copy(
            src_ref=bds.at[:, pl.ds(f * F, F)], dst_ref=nbr_bds.at[OPP[f]], send_sem=bs.at[f], recv_sem=br.at[OPP[f]],
            device_id=nbr[f], device_id_type=MESH,
        )

    when_each(lambda f: face_basis(f).start())

    def spread(axis, src_of, dst, send_sem, recv_sem):
        def send(i, _):
            if axis == "col":
                to = lax.rem(col + i, N)
                dev = (row, to)
            else:
                to = lax.rem(row + i, N)
                dev = (to, col)
            pltpu.make_async_remote_copy(
                src_ref=src_of(to), dst_ref=dst, send_sem=send_sem, recv_sem=recv_sem, device_id=dev, device_id_type=MESH
            ).start()
            return 0

        lax.fori_loop(1, N, send, 0)

    def wait_many(buf, sem):
        part = buf.at[pl.ds(0, N - 1)]
        pltpu.make_async_copy(part, part, sem).wait()

    crow[col] = cinv[...]
    spread("col", lambda to: cinv, crow.at[col], cs.at[0], cr.at[0])

    def chunk(rd, q):
        rows = F // CHUNKS

        def one(f):
            pltpu.make_async_remote_copy(
                src_ref=y.at[pl.ds(f * F + q * rows, rows)], dst_ref=halo.at[rd, OPP[f], pl.ds(q * rows, rows)],
                send_sem=hs.at[rd, f], recv_sem=hr.at[rd, OPP[f]], device_id=nbr[f], device_id_type=MESH,
            ).start()

        when_each(one)

    def halo_sent(rd):
        def one(f):
            part = y.at[pl.ds(f * F, F)]
            pltpu.make_async_copy(part, part, hs.at[rd, f]).wait()

        when_each(one)

    def halo_wait(rd, f):
        @pl.when(has[f])
        def _():
            part = halo.at[rd, f]
            pltpu.make_async_copy(part, part, hr.at[rd, f]).wait()

    get_load.wait()
    for f, perm in ((0, pn), (2, pw)):
        parts = split3(y[f * F : (f + 1) * F, :])
        hi, mid, lo = [mm(perm[...], part) for part in parts]
        y[f * F : (f + 1) * F, :] = (hi + mid) + lo
    vhi, vlo = split(y[...])
    uhi[...] = vhi
    ulo[...] = vlo

    def wait_basis(f):
        part = nbr_bds.at[f]
        pltpu.make_async_copy(part, part, br.at[f]).wait()

    when_each(wait_basis)
    bext[...] = jnp.zeros_like(bext)
    drow = []
    for f in range(4):
        at = slice(f * F, (f + 1) * F)
        bext[0:8, at] = wt[f] * bds[0:8, at]
        bext[8 + 8 * f : 16 + 8 * f, at] = wt[f] * nbr_bds[f, 0:8]
        drow.append((wt[f] * wt[f]) * (bds[8:9, at] + nbr_bds[f, 8:9]))
    bhi, blo = split(bext[...])
    bst[0:48] = bhi
    bst[48:96] = blo

    lane = lax.broadcasted_iota(jnp.int32, (8, 128), 1)
    lane_group = lax.shift_right_logical(lane, 4)
    sub = lax.broadcasted_iota(jnp.int32, (8, 128), 0)
    lane_sq = lax.broadcasted_iota(jnp.int32, (128, 128), 1)

    def contributions(rd, mat):
        both = mm(mat[...], uhi[...])
        c48 = both[0:48] + (both[48:96] + mm(mat[0:48], ulo[...]))
        for b in range(N):
            half, at = divmod(b, 8)
            tile = jnp.zeros((8, 128), f32)
            for g in range(5):
                piece = c48[8 * g : 8 * g + 8, 128 * half : 128 * half + 128]
                shift = (16 * (g - at)) % 128
                if shift:
                    piece = pltpu.roll(piece, shift, 1)
                tile = jnp.where(lane_group == g, piece, tile)
            p1s[rd, b] = tile
        p1r[rd, col] = p1s[rd, col]
        spread("col", lambda to: p1s.at[rd, to], p1r.at[rd, col], s1.at[rd], r1.at[rd])

    def neighbour_parts(rd):
        wait_many(p1r.at[rd], r1.at[rd])
        part = p1r[rd].reshape(128, 128)
        from_east = pltpu.roll(part, 80, 1)
        from_west = pltpu.roll(part, 64, 1)
        block = part + (
            jnp.concatenate([from_east[8:], from_east[:8]], axis=0)
            + jnp.concatenate([from_west[120:], from_west[:120]], axis=0)
        )
        turned = jnp.where(lane_sq < SB, block, part).T
        ns[rd] = turned[0:48]

        def send(f):
            pltpu.make_async_remote_copy(
                src_ref=ns.at[rd, pl.ds(SB * (f + 1), SB)], dst_ref=nr.at[rd, OPP[f]], send_sem=s15.at[rd, f],
                recv_sem=r15.at[rd, OPP[f]], device_id=nbr[f], device_id_type=MESH,
            ).start()

        when_each(send, (0, 1))

    def gather_rows(rd, dots):
        def wait(f):
            part = nr.at[rd, f]
            pltpu.make_async_copy(part, part, r15.at[rd, f]).wait()

        when_each(wait, (0, 1))
        p2s[rd, 0:SB] = ns[rd, 0:SB] + (nr[rd, 0] + nr[rd, 1])
        p2s[rd, SB : SB + 8] = dots
        p2r[rd, row] = p2s[rd]
        spread("row", lambda to: p2s.at[rd], p2r.at[rd, row], s2.at[rd], r2.at[rd])

    def sum_tiles(buf, rd, at):
        total = buf[rd, 0, at : at + 8]
        for i in range(1, N):
            total = total + buf[rd, i, at : at + 8]
        return total

    def solve(rd):
        wait_many(p2r.at[rd], r2.at[rd])
        rhs = jnp.concatenate([p2r[rd, i, 0:SB] for i in range(N)], axis=1)
        hi, lo = split(rhs)
        both = mm_nt(jnp.concatenate([hi, lo], axis=0), chi[...])
        solved = both[0:SB] + (both[SB : 2 * SB] + mm_nt(hi, clo[...]))
        tiles = jnp.concatenate(
            [solved, pltpu.roll(solved, 120, 1), pltpu.roll(solved, 8, 1), jnp.zeros((80, 128), f32)], axis=0
        ).T.reshape(N, 8, 128)
        dots = sum_tiles(p2r, rd, SB)
        for i in range(N):
            p3s[rd, i, 0:8] = tiles[i]
            p3s[rd, i, 8:16] = dots
        p3r[rd, col] = p3s[rd, col]
        spread("col", lambda to: p3s.at[rd, to], p3r.at[rd, col], s3.at[rd], r3.at[rd])

    def neighbour_solutions(rd):
        wait_many(p3r.at[rd], r3.at[rd])
        out = []
        for g in range(3):
            halves = []
            for half in range(2):
                total = jnp.zeros((8, 128), f32)
                for b in range(8):
                    piece = p3r[rd, 8 * half + b, 0:8]
                    shift = (16 * (b - g)) % 128
                    if shift:
                        piece = pltpu.roll(piece, shift, 1)
                    total = jnp.where(lane_group == b, piece, total)
                halves.append(total)
            out.append(jnp.concatenate(halves, axis=1))
        ts[rd] = out[0]

        def send(f):
            pltpu.make_async_remote_copy(
                src_ref=ts.at[rd], dst_ref=tr.at[rd, OPP[f]], send_sem=s35.at[rd, f], recv_sem=r35.at[rd, OPP[f]],
                device_id=nbr[f], device_id_type=MESH,
            ).start()

        when_each(send, (0, 1))
        return out, sum_tiles(p3r, rd, 8)

    def extended_solution(rd, own):
        def wait(f):
            part = tr.at[rd, f]
            pltpu.make_async_copy(part, part, r35.at[rd, f]).wait()

        when_each(wait, (0, 1))
        return jnp.concatenate([own[0], tr[rd, 0], tr[rd, 1], own[2], own[1]], axis=0)

    def set_tau(new):
        tau[...] = new
        hi = new.astype(bf16).astype(f32)
        tcat[0:40] = hi.astype(bf16)
        tcat[64:104] = (new - hi).astype(bf16)
        tcat[128:168] = hi.astype(bf16)

    def dot_tile(delta, gamma, eps):
        tile = jnp.zeros((8, 128), f32)
        for i, v in enumerate((delta, gamma, eps)):
            if v is not None:
                tile = jnp.where(sub == 2 * i, v[:, 0:128], tile)
                tile = jnp.where(sub == 2 * i + 1, v[:, 128:256], tile)
        return tile

    def scalars(tile):
        return [jnp.concatenate([tile[2 * i : 2 * i + 1], tile[2 * i + 1 : 2 * i + 2]], axis=1) for i in range(3)]

    def prepare_rows(f):
        at = slice(f * F, (f + 1) * F)
        parts = list(split(smat[at, :]))
        for part, dst in zip(parts, (shi, slo)):
            if f == 0:
                part = mm(pn[...], part).astype(bf16)
            elif f == 2:
                part = mm(pw[...], part).astype(bf16)
            dst[at, 0:F] = mm_nt(part[:, 0:F], pn[...]).astype(bf16)
            dst[at, F : 2 * F] = part[:, F : 2 * F]
            dst[at, 2 * F : 3 * F] = mm_nt(part[:, 2 * F : 3 * F], pw[...]).astype(bf16)
            dst[at, 3 * F :] = part[:, 3 * F :]

    def new_u(f):
        at = slice(f * F, (f + 1) * F)
        d = dcol[at, :]
        res = r[at, :]
        val = jnp.concatenate([d, d], axis=1) * res + mm(bcat[at, :], tcat[...])
        u[at, :] = val
        hi, lo = split(val)
        uhi[at, :] = hi
        ulo[at, :] = lo
        return wt[f] * jnp.sum(res * val, axis=0, keepdims=True), val

    def apply_schur():
        delta = jnp.zeros((1, SC), f32)

        def block(f, total):
            at = pl.ds(pl.multiple_of(f * F, F), F)
            val = mm(shi[at, :], uhi[...]) + (mm(shi[at, :], ulo[...]) + mm(slo[at, :], uhi[...]))
            y[at, :] = val
            return total + jnp.sum(u[at, :] * val, axis=0, keepdims=True)

        return lax.fori_loop(0, 4, block, delta)

    contributions(0, bst)
    chunk(0, 0)
    get_s.wait()
    prepare_rows(0)
    prepare_rows(1)
    neighbour_parts(0)
    chunk(0, 1)
    prepare_rows(2)
    gather_rows(0, jnp.zeros((8, 128), f32))
    chunk(0, 2)
    prepare_rows(3)
    wait_many(crow, cr.at[0])
    chi_v, clo_v = split(crow[...].reshape(128, N * 128))
    chi[...] = chi_v
    clo[...] = clo_v
    solve(0)
    chunk(0, 3)
    both = mm(bst[...], shi[...])
    gt = both[0:48] + (both[48:96] + mm(bst[0:48], slo[...]))
    ghi, glo = split(gt)
    gst[0:48] = ghi
    gst[48:96] = glo
    tcat[...] = jnp.zeros_like(tcat)
    bhi32 = bext[...].astype(bf16).astype(f32)
    blo32 = bext[...] - bhi32
    pad = jnp.zeros((16, NI), f32)
    bcat[...] = jnp.concatenate([bhi32, pad, bhi32, pad, blo32, pad, jnp.zeros((64, NI), f32)], axis=0).T.astype(bf16)
    dcol[...] = jnp.broadcast_to(jnp.concatenate(drow, axis=1), (128, NI)).T
    own, _ = neighbour_solutions(0)
    set_tau(extended_solution(0, own))
    gamma = jnp.zeros((1, SC), f32)
    for f in (3, 2, 1, 0):
        at = slice(f * F, (f + 1) * F)
        halo_wait(0, f)
        r[at, :] = y[at, :] + halo[0, f]
        gamma = gamma + new_u(f)[0]
    halo_sent(0)

    eps = None
    gamma_old = pap_old = None
    for rd in range(1, ROUNDS):
        last = rd == ROUNDS - 1
        if not last:
            contributions(rd, gst)
        delta = apply_schur()
        dots = dot_tile(delta, gamma, eps)
        if not last:
            chunk(rd, 0)
            neighbour_parts(rd)
            chunk(rd, 1)
            gather_rows(rd, dots)
            chunk(rd, 2)
            solve(rd)
            chunk(rd, 3)
            own, total = neighbour_solutions(rd)
        else:
            p2s[rd, SB : SB + 8] = dots
            p2r[rd, row, SB : SB + 8] = dots
            spread("row", lambda to: p2s.at[rd, pl.ds(SB, 8)], p2r.at[rd, row, pl.ds(SB, 8)], s2.at[rd], r2.at[rd])
            for q in range(CHUNKS - 1):
                chunk(rd, q)
            wait_many(p2r.at[rd, :, pl.ds(SB, 8)], r2.at[rd])
            dots = sum_tiles(p2r, rd, SB)
            p3s[rd, 0, 8:16] = dots
            p3r[rd, col, 8:16] = dots
            spread("col", lambda to: p3s.at[rd, 0, pl.ds(8, 8)], p3r.at[rd, col, pl.ds(8, 8)], s3.at[rd], r3.at[rd])
            chunk(rd, CHUNKS - 1)
            wait_many(p3r.at[rd, :, pl.ds(8, 8)], r3.at[rd])
            total = sum_tiles(p3r, rd, 8)
        delta_t, gamma_t, eps_t = scalars(total)
        if rd == 1:
            beta = None
            pap = delta_t
        else:
            beta = gamma_t / gamma_old
            pap = delta_t + beta * (2.0 * eps_t + beta * pap_old)
        alpha = gamma_t / pap
        gamma_old, pap_old = gamma_t, pap
        if not last:
            solved = extended_solution(rd, own)
            if beta is not None:
                solved = solved + beta * sig[...]
            sig[...] = solved
            set_tau(tau[...] - alpha * solved)
        gamma = jnp.zeros((1, SC), f32)
        eps = jnp.zeros((1, SC), f32)
        for f in (3, 2, 1, 0):
            at = slice(f * F, (f + 1) * F)
            halo_wait(rd, f)
            direction = u[at, :]
            image = y[at, :] + halo[rd, f]
            if beta is not None:
                direction = direction + beta * p[at, :]
                image = image + beta * s[at, :]
            iterate = alpha * direction
            if beta is not None:
                iterate = iterate + x[at, :]
            res = r[at, :] - alpha * image
            if not last:
                x[at, :] = iterate
                r[at, :] = res
                p[at, :] = direction
                s[at, :] = image
                share, val = new_u(f)
                gamma = gamma + share
                eps = eps + wt[f] * jnp.sum(val * image, axis=0, keepdims=True)
            else:
                for val, dst in ((iterate, sol_out), (res, res_out)):
                    if f in (0, 2):
                        perm = (pn if f == 0 else pw)[...]
                        hi, mid, lo = [
                            lax.dot_general(perm, part, (((0,), (0,)), ((), ())), preferred_element_type=f32)
                            for part in split3(val)
                        ]
                        val = (hi + mid) + lo
                    dst[at, :] = val
        halo_sent(rd)

    when_each(lambda f: face_basis(f).wait_send())
    wait_many(crow, cs.at[0])
    for rd in range(ROUNDS):
        if rd < ROUNDS - 1:
            wait_many(p1r.at[rd], s1.at[rd])
            wait_many(p2r.at[rd], s2.at[rd])
            wait_many(p3r.at[rd], s3.at[rd])

            def sent(f):
                part = nr.at[rd, f]
                pltpu.make_async_copy(part, part, s15.at[rd, f]).wait()
                part = tr.at[rd, f]
                pltpu.make_async_copy(part, part, s35.at[rd, f]).wait()

            when_each(sent, (0, 1))
        else:
            wait_many(p2r.at[rd, :, pl.ds(SB, 8)], s2.at[rd])
            wait_many(p3r.at[rd, :, pl.ds(8, 8)], s3.at[rd])


def body(schur, load, dscale, basis, coarse_inv, north_match, west_match):
    vmem = pl.BlockSpec(memory_space=pltpu.VMEM)
    anywhere = pl.BlockSpec(memory_space=pl.ANY)
    dma = pltpu.SemaphoreType.DMA

    def buf(*shape, dtype=f32):
        return pltpu.VMEM(shape, dtype)

    vec = buf(NI, SC)
    half = buf(NI, SC, dtype=bf16)
    solved, left = pl.pallas_call(
        kernel,
        out_shape=[jax.ShapeDtypeStruct((NI, SC), f32)] * 2,
        in_specs=[anywhere, anywhere] + [vmem] * 5,
        out_specs=[vmem, vmem],
        scratch_shapes=[
            buf(NI, NI), buf(NI, NI, dtype=bf16), buf(NI, NI, dtype=bf16),
            vec, vec, vec, vec, vec, vec, half, half, buf(NI, 128),
            buf(F, F, dtype=bf16), buf(F, F, dtype=bf16), buf(16, NI), buf(4, 16, F), buf(48, NI),
            buf(96, NI, dtype=bf16), buf(96, NI, dtype=bf16), buf(NI, 256, dtype=bf16), buf(256, SC, dtype=bf16),
            buf(40, SC), buf(40, SC),
            buf(N, K, N * 128), buf(128, N * 128, dtype=bf16), buf(128, N * 128, dtype=bf16),
            buf(ROUNDS, 4, F, SC),
            buf(ROUNDS, N, 8, 128), buf(ROUNDS, N, 8, 128),
            buf(ROUNDS, 48, 128), buf(ROUNDS, 2, SB, 128),
            buf(ROUNDS, SB + 8, 128), buf(ROUNDS, N, SB + 8, 128),
            buf(ROUNDS, N, 16, 128), buf(ROUNDS, N, 16, 128),
            buf(ROUNDS, K, SC), buf(ROUNDS, 2, K, SC),
            dma((2,)), dma((ROUNDS, 4)), dma((ROUNDS, 4)), dma((4,)), dma((4,)), dma((1,)), dma((1,)),
            dma((ROUNDS,)), dma((ROUNDS,)), dma((ROUNDS, 2)), dma((ROUNDS, 2)), dma((ROUNDS,)), dma((ROUNDS,)),
            dma((ROUNDS,)), dma((ROUNDS,)), dma((ROUNDS, 2)), dma((ROUNDS, 2)),
        ],
        compiler_params=pltpu.CompilerParams(collective_id=0, has_side_effects=True, vmem_limit_bytes=52 << 20),
    )(
        schur.reshape(NI, NI), load.reshape(NI, SC), dscale.reshape(1, NI), basis.reshape(K, NI),
        coarse_inv, north_match.reshape(1, F), west_match.reshape(1, F),
    )
    return solved.reshape(1, 1, NI, SC), left.reshape(1, 1, NI, SC)


def solution(mesh):
    placed = (
        P("row", "col", None, None),
        P("row", "col", None, None),
        P("row", "col", None),
        P("row", "col", None, None),
        P(("row", "col"), None),
        P("row", "col", None),
        P("row", "col", None),
    )
    return jax.shard_map(
        body,
        mesh=mesh,
        in_specs=placed,
        out_specs=(P("row", "col", None, None), P("row", "col", None, None)),
        check_vma=False,
    )
```

```python
import functools

import jax
import jax.numpy as jnp
from jax import lax
from jax.experimental import pallas as pl
from jax.experimental.pallas import tpu as pltpu
from jax.sharding import PartitionSpec as P

MESH = pl.DeviceIdType.MESH
F = 256
NI = 1024
SC = 256
K = 8
N = 16
SB = 16
ROUNDS = 4
CUTS = (0, 80, 176, 256)
OPP = (1, 0, 3, 2)
f32, bf16 = jnp.float32, jnp.bfloat16
NT = (((1,), (1,)), ((), ()))


def mm(a, b):
    return jnp.dot(a, b, preferred_element_type=f32)


def mm_nt(a, b):
    return lax.dot_general(a, b, NT, preferred_element_type=f32)


def split(x):
    hi = x.astype(bf16)
    return hi, (x - hi.astype(f32)).astype(bf16)


def split3(x):
    hi = x.astype(bf16)
    rest = x - hi.astype(f32)
    mid = rest.astype(bf16)
    return hi, mid, (rest - mid.astype(f32)).astype(bf16)


def kernel(
    schur_in, load_in, dscale_in, basis_in, cinv_in, north_in, west_in,
    sol_out, res_out,
    dscale, north, west,
    smat, shi, slo, y, u, r, p, s, x, uhi, ulo, dcol,
    pn, pw, bds, nbr_bds, bext, bst, gst, bcat, tcat, tau, sig,
    crow, chi, clo,
    halo, p1s, p1r, p1ns, p1nr, p2s, p2r, p3s, p3r, p3ns, p3nr, pm,
    local_sem, hs, hr, bs, br, cs, cr, s1, r1, s2, r2, s3, r3,
):
    row, col = lax.axis_index("row"), lax.axis_index("col")
    has = (row > 0, row < N - 1, col > 0, col < N - 1)
    nbr = ((row - 1, col), (row + 1, col), (row, col - 1), (row, col + 1))
    wt = [jnp.where(h, 0.5, 1.0).astype(f32) for h in has]

    def fetch(i, src, dst):
        copy = pltpu.make_async_copy(src, dst, local_sem.at[i])
        copy.start()
        return copy

    get_small = [
        fetch(0, north_in, north), fetch(1, west_in, west), fetch(2, basis_in, bds.at[pl.ds(0, 8)]), fetch(3, dscale_in, dscale),
    ]
    get_cinv = fetch(4, cinv_in, crow.at[col])
    get_load = fetch(5, load_in, y)
    get_s = fetch(6, schur_in, smat)

    barrier = pltpu.get_barrier_semaphore()

    def greet(i, _):
        pl.semaphore_signal(barrier, inc=1, device_id=(lax.rem(row + i, N), col), device_id_type=MESH)
        for step in (0, 1, N - 1):
            other = (lax.rem(row + step, N), lax.rem(col + i, N))
            pl.semaphore_signal(barrier, inc=1, device_id=other, device_id_type=MESH)
        return 0

    lax.fori_loop(1, N, greet, 0)

    for copy in get_small:
        copy.wait()

    slot = lax.broadcasted_iota(jnp.int32, (F, F), 0)
    pn[...] = jnp.where(slot == north[...], 1.0, 0.0).astype(bf16)
    pw[...] = jnp.where(slot == west[...], 1.0, 0.0).astype(bf16)

    for f in range(4):

        @pl.when(jnp.logical_not(has[f]))
        def _():
            nbr_bds[f] = jnp.zeros((16, F), f32)
            for rd in range(ROUNDS):
                halo[rd, f] = jnp.zeros((F, SC), f32)
            if f < 2:
                for rd in range(ROUNDS - 1):
                    p1nr[rd, f] = jnp.zeros((N, 1, 128), f32)
                    p3nr[rd, f] = jnp.zeros((N, 1, 128), f32)

    bds[8:16] = jnp.where(lax.broadcasted_iota(jnp.int32, (8, NI), 0) == 0, dscale[...], 0.0)
    for f, perm in ((0, pn), (2, pw)):
        parts = split3(bds[:, f * F : (f + 1) * F])
        hi, mid, lo = [mm_nt(part, perm[...]) for part in parts]
        bds[:, f * F : (f + 1) * F] = (hi + mid) + lo

    pl.semaphore_wait(barrier, 4 * (N - 1))

    def when_each(fn, faces=(0, 1, 2, 3)):
        for f in faces:
            pl.when(has[f])(functools.partial(fn, f))

    def face_basis(f):
        return pltpu.make_async_remote_copy(
            src_ref=bds.at[:, pl.ds(f * F, F)], dst_ref=nbr_bds.at[OPP[f]], send_sem=bs.at[f], recv_sem=br.at[OPP[f]],
            device_id=nbr[f], device_id_type=MESH,
        )

    when_each(lambda f: face_basis(f).start())

    def copy_to(src, dst, send_sem, recv_sem, dev):
        return pltpu.make_async_remote_copy(
            src_ref=src, dst_ref=dst, send_sem=send_sem, recv_sem=recv_sem, device_id=dev, device_id_type=MESH
        )

    def along_col(first, up, src_of, dst, send_sem, recv_sem):
        def send(i, _):
            to = lax.rem(col + i, N)
            copy_to(src_of(to), dst, send_sem, recv_sem, (row - up, to)).start()
            return 0

        lax.fori_loop(first, N, send, 0)

    def three_rows(up_src, down_src, up_dst, down_dst, src_of, dst, send_sem, recv_sem):
        pl.when(has[0])(lambda: along_col(0, 1, lambda to: up_src.at[to], up_dst.at[col], send_sem.at[1], recv_sem.at[2]))
        pl.when(has[1])(lambda: along_col(0, -1, lambda to: down_src.at[to], down_dst.at[col], send_sem.at[2], recv_sem.at[1]))
        along_col(1, 0, src_of, dst, send_sem.at[0], recv_sem.at[0])

    def along_row(src, dst, send_sem, recv_sem):
        def send(i, _):
            copy_to(src, dst, send_sem, recv_sem, (lax.rem(row + i, N), col)).start()
            return 0

        lax.fori_loop(1, N, send, 0)

    def wait_many(buf, sem, count=N - 1):
        part = buf.at[pl.ds(0, count)]
        pltpu.make_async_copy(part, part, sem).wait()

    def three_waits(own, other, sem):
        wait_many(own, sem.at[0])
        for f in (0, 1):
            pl.when(has[f])(functools.partial(wait_many, other.at[f], sem.at[f + 1], N))

    get_cinv.wait()
    mine = crow.at[col]

    def send_cinv(i, _):
        copy_to(mine, mine, cs.at[0], cr.at[0], (row, lax.rem(col + 2 * i, N))).start()
        return 0

    lax.fori_loop(1, N // 2, send_cinv, 0)
    partner = col + 1 - 2 * lax.rem(col, 2)

    def pass_cinv():
        wait_many(crow, cr.at[0], N // 2 - 1)

        def send(i, _):
            block = crow.at[2 * i + lax.rem(col, 2)]
            copy_to(block, block, cs.at[1], cr.at[1], (row, partner)).start()
            return 0

        lax.fori_loop(0, N // 2, send, 0)

    def chunk(rd, q):
        start, rows = CUTS[q], CUTS[q + 1] - CUTS[q]

        def one(f):
            pltpu.make_async_remote_copy(
                src_ref=y.at[pl.ds(f * F + start, rows)], dst_ref=halo.at[rd, OPP[f], pl.ds(start, rows)],
                send_sem=hs.at[rd, f], recv_sem=hr.at[rd, OPP[f]], device_id=nbr[f], device_id_type=MESH,
            ).start()

        when_each(one)

    def halo_sent(rd):
        def one(f):
            part = y.at[pl.ds(f * F, F)]
            pltpu.make_async_copy(part, part, hs.at[rd, f]).wait()

        when_each(one)

    def halo_wait(rd, f):
        @pl.when(has[f])
        def _():
            part = halo.at[rd, f]
            pltpu.make_async_copy(part, part, hr.at[rd, f]).wait()

    get_load.wait()
    for f, perm in ((0, pn), (2, pw)):
        parts = split3(y[f * F : (f + 1) * F, :])
        hi, mid, lo = [mm(perm[...], part) for part in parts]
        y[f * F : (f + 1) * F, :] = (hi + mid) + lo
    vhi, vlo = split(y[...])
    uhi[...] = vhi
    ulo[...] = vlo

    def wait_basis(f):
        part = nbr_bds.at[f]
        pltpu.make_async_copy(part, part, br.at[f]).wait()

    when_each(wait_basis)
    bext[...] = jnp.zeros_like(bext)
    drow = []
    for f in range(4):
        at = slice(f * F, (f + 1) * F)
        bext[0:8, at] = wt[f] * bds[0:8, at]
        bext[8 + 8 * f : 16 + 8 * f, at] = wt[f] * nbr_bds[f, 0:8]
        drow.append((wt[f] * wt[f]) * (bds[8:9, at] + nbr_bds[f, 8:9]))
    bhi, blo = split(bext[...])
    bst[0:48] = bhi
    bst[48:96] = blo

    lane = lax.broadcasted_iota(jnp.int32, (8, 128), 1)
    lane_group = lax.shift_right_logical(lane, 4)
    sub = lax.broadcasted_iota(jnp.int32, (8, 128), 0)
    lane_group16 = lax.shift_right_logical(lax.broadcasted_iota(jnp.int32, (SB, 128), 1), 4)
    diagonal = jnp.bitwise_and(lane_group - sub, 7)

    def turn(tile):
        out = tile
        for d in range(1, 8):
            out = jnp.where(diagonal == d, pltpu.roll(pltpu.roll(tile, SB * d, 1), 8 - d, 0), out)
        return out

    def to_blocks(part):
        return jnp.concatenate([turn(part[:, 0:128]), turn(part[:, 128:256])], axis=0)

    def from_blocks(part):
        return jnp.concatenate([turn(part[0:8]), turn(part[8:16])], axis=1)

    def rows_tile(rows):
        tile = jnp.zeros((8, 128), f32)
        for i, v in enumerate(rows):
            tile = jnp.where(sub == i, v, tile)
        return tile


    def contributions(rd, mat):
        both = mm(mat[...], uhi[...])
        c48 = both[0:48] + (both[48:96] + mm(mat[0:48], ulo[...]))
        own, north_part, south_part, west_part, east_part = [to_blocks(c48[8 * g : 8 * g + 8]) for g in range(5)]
        p1ns[rd, 0] = north_part.reshape(N, 1, 128)
        p1ns[rd, 1] = south_part.reshape(N, 1, 128)
        for b in range(N):
            p1s[rd, b] = rows_tile([part[b : b + 1] for part in (own, west_part, east_part)])
        p1r[rd, col] = p1s[rd, col]
        three_rows(
            p1ns.at[rd, 0], p1ns.at[rd, 1], p1nr.at[rd, 1], p1nr.at[rd, 0], lambda to: p1s.at[rd, to], p1r.at[rd, col],
            s1.at[rd], r1.at[rd],
        )

    def up_one(a):
        return jnp.concatenate([a[1:], a[:1]], axis=0)

    def down_one(a):
        return jnp.concatenate([a[N - 1 :], a[: N - 1]], axis=0)

    def gather_rows(rd, dots):
        three_waits(p1r.at[rd], p1nr.at[rd], r1.at[rd])
        own, west_part, east_part = [
            jnp.concatenate([p1r[rd, i, g : g + 1] for i in range(N)], axis=0) for g in range(3)
        ]
        block = (own + (p1nr[rd, 0].reshape(N, 128) + p1nr[rd, 1].reshape(N, 128))) + (up_one(west_part) + down_one(east_part))
        turned = jnp.concatenate([block, jnp.zeros((128 - N, 128), f32)], axis=0).T
        rhs = turned[0:SB]
        for k in range(1, K):
            rhs = jnp.where(lane_group16 == k, pltpu.roll(turned[SB * k : SB * k + SB], SB * k, 1), rhs)
        p2s[rd, 0:SB] = rhs
        p2s[rd, SB : SB + 8] = dots
        p2r[rd, row] = p2s[rd]
        along_row(p2s.at[rd], p2r.at[rd, row], s2.at[rd], r2.at[rd])

    def sum_tiles(buf, at):
        total = buf[0, at : at + 8]
        for i in range(1, N):
            total = total + buf[i, at : at + 8]
        return total

    def solve(rd):
        wait_many(p2r.at[rd], r2.at[rd])
        rhs = jnp.concatenate([p2r[rd, i, 0:SB] for i in range(N)], axis=1)
        hi, lo = split(rhs)
        both = mm_nt(jnp.concatenate([hi, lo], axis=0), chi[...])
        solved = both[0:SB] + (both[SB : 2 * SB] + mm_nt(hi, clo[...]))
        pieces = [solved] + [pltpu.roll(solved, 128 - SB * k, 1) for k in range(1, K)]
        own = jnp.concatenate(pieces, axis=0).T[0:N]
        east_of, west_of = up_one(own), down_one(own)
        dots = sum_tiles(p2r.at[rd], SB)
        p3ns[rd] = own.reshape(N, 1, 128)
        for i in range(N):
            p3s[rd, i, 0:8] = rows_tile([part[i : i + 1] for part in (own, west_of, east_of)])
            p3s[rd, i, 8:16] = dots
        p3r[rd, col] = p3s[rd, col]
        three_rows(
            p3ns.at[rd], p3ns.at[rd], p3nr.at[rd, 1], p3nr.at[rd, 0], lambda to: p3s.at[rd, to], p3r.at[rd, col],
            s3.at[rd], r3.at[rd],
        )

    def solutions(rd):
        three_waits(p3r.at[rd], p3nr.at[rd], r3.at[rd])
        own, west_of, east_of = [jnp.concatenate([p3r[rd, i, g : g + 1] for i in range(N)], axis=0) for g in range(3)]
        parts = [own, p3nr[rd, 0].reshape(N, 128), p3nr[rd, 1].reshape(N, 128), west_of, east_of]
        return jnp.concatenate([from_blocks(part) for part in parts], axis=0), sum_tiles(p3r.at[rd], 8)

    def set_tau(new):
        tau[...] = new
        hi = new.astype(bf16).astype(f32)
        tcat[0:40] = hi.astype(bf16)
        tcat[64:104] = (new - hi).astype(bf16)
        tcat[128:168] = hi.astype(bf16)

    def dot_tile(delta, gamma, eps):
        tile = jnp.zeros((8, 128), f32)
        for i, v in enumerate((delta, gamma, eps)):
            if v is not None:
                tile = jnp.where(sub == 2 * i, v[:, 0:128], tile)
                tile = jnp.where(sub == 2 * i + 1, v[:, 128:256], tile)
        return tile

    def scalars(tile):
        return [jnp.concatenate([tile[2 * i : 2 * i + 1], tile[2 * i + 1 : 2 * i + 2]], axis=1) for i in range(3)]

    def prepare_rows(f):
        at = slice(f * F, (f + 1) * F)
        parts = list(split(smat[at, :]))
        for part, dst in zip(parts, (shi, slo)):
            if f == 0:
                part = mm(pn[...], part).astype(bf16)
            elif f == 2:
                part = mm(pw[...], part).astype(bf16)
            dst[at, 0:F] = mm_nt(part[:, 0:F], pn[...]).astype(bf16)
            dst[at, F : 2 * F] = part[:, F : 2 * F]
            dst[at, 2 * F : 3 * F] = mm_nt(part[:, 2 * F : 3 * F], pw[...]).astype(bf16)
            dst[at, 3 * F :] = part[:, 3 * F :]

    def new_u(f):
        at = slice(f * F, (f + 1) * F)
        d = dcol[at, :]
        res = r[at, :]
        val = jnp.concatenate([d, d], axis=1) * res + mm(bcat[at, :], tcat[...])
        u[at, :] = val
        hi, lo = split(val)
        uhi[at, :] = hi
        ulo[at, :] = lo
        return wt[f] * jnp.sum(res * val, axis=0, keepdims=True), val

    def own_order(f, val):
        if f in (1, 3):
            return val
        perm = (pn if f == 0 else pw)[...]
        hi, mid, lo = [
            lax.dot_general(perm, part, (((0,), (0,)), ((), ())), preferred_element_type=f32) for part in split3(val)
        ]
        return (hi + mid) + lo

    def apply_schur():
        delta = jnp.zeros((1, SC), f32)

        def block(f, total):
            at = pl.ds(pl.multiple_of(f * F, F), F)
            val = mm(shi[at, :], uhi[...]) + (mm(shi[at, :], ulo[...]) + mm(slo[at, :], uhi[...]))
            y[at, :] = val
            return total + jnp.sum(u[at, :] * val, axis=0, keepdims=True)

        return lax.fori_loop(0, 4, block, delta)

    contributions(0, bst)
    chunk(0, 0)
    get_s.wait()
    prepare_rows(0)
    prepare_rows(1)
    gather_rows(0, jnp.zeros((8, 128), f32))
    pass_cinv()
    chunk(0, 1)
    prepare_rows(2)
    prepare_rows(3)
    wait_many(crow, cr.at[1], N // 2)
    order = lax.broadcasted_iota(jnp.int32, (128, 128), 0)
    order = jnp.bitwise_and(order, N - 1) * K + lax.shift_right_logical(order, 4)
    pm[...] = jnp.where(order == lax.broadcasted_iota(jnp.int32, (128, 128), 1), 1.0, 0.0).astype(bf16)
    for part, dst in zip(split(crow[...].reshape(128, N * 128)), (chi, clo)):
        part = mm(pm[...], part).astype(bf16)
        for i in range(N):
            dst[:, i * 128 : i * 128 + 128] = mm_nt(part[:, i * 128 : i * 128 + 128], pm[...]).astype(bf16)
    solve(0)
    chunk(0, 2)
    both = mm(bst[...], shi[...])
    gt = both[0:48] + (both[48:96] + mm(bst[0:48], slo[...]))
    ghi, glo = split(gt)
    gst[0:48] = ghi
    gst[48:96] = glo
    tcat[...] = jnp.zeros_like(tcat)
    bhi32 = bext[...].astype(bf16).astype(f32)
    blo32 = bext[...] - bhi32
    pad = jnp.zeros((16, NI), f32)
    bcat[...] = jnp.concatenate([bhi32, pad, bhi32, pad, blo32, pad, jnp.zeros((64, NI), f32)], axis=0).T.astype(bf16)
    dcol[...] = jnp.broadcast_to(jnp.concatenate(drow, axis=1), (128, NI)).T
    set_tau(solutions(0)[0])
    gamma = jnp.zeros((1, SC), f32)
    for f in (3, 2, 1, 0):
        at = slice(f * F, (f + 1) * F)
        halo_wait(0, f)
        r[at, :] = y[at, :] + halo[0, f]
        gamma = gamma + new_u(f)[0]
    halo_sent(0)

    eps = None
    gamma_old = pap_old = None
    for rd in range(1, ROUNDS):
        last = rd == ROUNDS - 1
        if not last:
            contributions(rd, gst)
        delta = apply_schur()
        dots = dot_tile(delta, gamma, eps)
        if not last:
            chunk(rd, 0)
            gather_rows(rd, dots)
            chunk(rd, 1)
            solve(rd)
            chunk(rd, 2)
            solved, total = solutions(rd)
        else:
            p2s[rd, SB : SB + 8] = dots
            p2r[rd, row, SB : SB + 8] = dots
            along_row(p2s.at[rd, pl.ds(SB, 8)], p2r.at[rd, row, pl.ds(SB, 8)], s2.at[rd], r2.at[rd])
            chunk(rd, 0)
            chunk(rd, 1)
            wait_many(p2r.at[rd, :, pl.ds(SB, 8)], r2.at[rd])
            dots = sum_tiles(p2r.at[rd], SB)
            p3s[rd, 0, 8:16] = dots
            p3r[rd, col, 8:16] = dots
            along_col(1, 0, lambda to: p3s.at[rd, 0, pl.ds(8, 8)], p3r.at[rd, col, pl.ds(8, 8)], s3.at[rd, 0], r3.at[rd, 0])
            chunk(rd, 2)
            wait_many(p3r.at[rd, :, pl.ds(8, 8)], r3.at[rd, 0])
            total = sum_tiles(p3r.at[rd], 8)
        delta_t, gamma_t, eps_t = scalars(total)
        if rd == 1:
            beta = None
            pap = delta_t
        else:
            beta = gamma_t / gamma_old
            pap = delta_t + beta * (2.0 * eps_t + beta * pap_old)
        alpha = gamma_t / pap
        gamma_old, pap_old = gamma_t, pap
        if not last:
            if beta is not None:
                solved = solved + beta * sig[...]
            sig[...] = solved
            set_tau(tau[...] - alpha * solved)
        for f in range(4):
            at = slice(f * F, (f + 1) * F)
            direction = u[at, :]
            if beta is not None:
                direction = direction + beta * p[at, :]
            iterate = alpha * direction
            if beta is not None:
                iterate = iterate + x[at, :]
            if last:
                sol_out[at, :] = own_order(f, iterate)
            else:
                p[at, :] = direction
                x[at, :] = iterate
        gamma = jnp.zeros((1, SC), f32)
        eps = jnp.zeros((1, SC), f32)
        for f in (3, 2, 1, 0):
            at = slice(f * F, (f + 1) * F)
            halo_wait(rd, f)
            image = y[at, :] + halo[rd, f]
            if beta is not None:
                image = image + beta * s[at, :]
            res = r[at, :] - alpha * image
            if last:
                res_out[at, :] = own_order(f, res)
            else:
                r[at, :] = res
                s[at, :] = image
                share, val = new_u(f)
                gamma = gamma + share
                eps = eps + wt[f] * jnp.sum(val * image, axis=0, keepdims=True)
        halo_sent(rd)

    when_each(lambda f: face_basis(f).wait_send())
    wait_many(crow, cs.at[0], N // 2 - 1)
    wait_many(crow, cs.at[1], N // 2)
    for rd in range(ROUNDS):
        if rd < ROUNDS - 1:
            three_waits(p1r.at[rd], p1nr.at[rd], s1.at[rd])
            wait_many(p2r.at[rd], s2.at[rd])
            three_waits(p3r.at[rd], p3nr.at[rd], s3.at[rd])
        else:
            wait_many(p2r.at[rd, :, pl.ds(SB, 8)], s2.at[rd])
            wait_many(p3r.at[rd, :, pl.ds(8, 8)], s3.at[rd, 0])


def body(schur, load, dscale, basis, coarse_inv, north_match, west_match):
    vmem = pl.BlockSpec(memory_space=pltpu.VMEM)
    hbm = pl.BlockSpec(memory_space=pltpu.HBM)
    dma = pltpu.SemaphoreType.DMA

    def buf(*shape, dtype=f32):
        return pltpu.VMEM(shape, dtype)

    vec = buf(NI, SC)
    half = buf(NI, SC, dtype=bf16)
    solved, left = pl.pallas_call(
        kernel,
        out_shape=[jax.ShapeDtypeStruct((NI, SC), f32)] * 2,
        in_specs=[hbm] * 7,
        out_specs=[vmem, vmem],
        scratch_shapes=[
            buf(1, NI), buf(1, F, dtype=jnp.int32), buf(1, F, dtype=jnp.int32),
            buf(NI, NI), buf(NI, NI, dtype=bf16), buf(NI, NI, dtype=bf16),
            vec, vec, vec, vec, vec, vec, half, half, buf(NI, 128),
            buf(F, F, dtype=bf16), buf(F, F, dtype=bf16), buf(16, NI), buf(4, 16, F), buf(48, NI),
            buf(96, NI, dtype=bf16), buf(96, NI, dtype=bf16), buf(NI, 256, dtype=bf16), buf(256, SC, dtype=bf16),
            buf(40, SC), buf(40, SC),
            buf(N, K, N * 128), buf(128, N * 128, dtype=bf16), buf(128, N * 128, dtype=bf16),
            buf(ROUNDS, 4, F, SC),
            buf(ROUNDS, N, 8, 128), buf(ROUNDS, N, 8, 128), buf(ROUNDS, 2, N, 1, 128), buf(ROUNDS, 2, N, 1, 128),
            buf(ROUNDS, SB + 8, 128), buf(ROUNDS, N, SB + 8, 128),
            buf(ROUNDS, N, 16, 128), buf(ROUNDS, N, 16, 128), buf(ROUNDS, N, 1, 128), buf(ROUNDS, 2, N, 1, 128),
            buf(128, 128, dtype=bf16),
            dma((7,)), dma((ROUNDS, 4)), dma((ROUNDS, 4)), dma((4,)), dma((4,)), dma((2,)), dma((2,)),
            dma((ROUNDS, 3)), dma((ROUNDS, 3)), dma((ROUNDS,)), dma((ROUNDS,)), dma((ROUNDS, 3)), dma((ROUNDS, 3)),
        ],
        compiler_params=pltpu.CompilerParams(collective_id=0, has_side_effects=True, vmem_limit_bytes=52 << 20),
    )(
        schur.reshape(NI, NI), load.reshape(NI, SC), dscale.reshape(1, NI), basis.reshape(K, NI),
        coarse_inv, north_match.reshape(1, F), west_match.reshape(1, F),
    )
    return solved.reshape(1, 1, NI, SC), left.reshape(1, 1, NI, SC)


def solution(mesh):
    placed = (
        P("row", "col", None, None),
        P("row", "col", None, None),
        P("row", "col", None),
        P("row", "col", None, None),
        P(("row", "col"), None),
        P("row", "col", None),
        P("row", "col", None),
    )
    return jax.shard_map(
        body,
        mesh=mesh,
        in_specs=placed,
        out_specs=(P("row", "col", None, None), P("row", "col", None, None)),
        check_vma=False,
    )
```

```python
import functools

import jax
import jax.numpy as jnp
from jax import lax
from jax.experimental import pallas as pl
from jax.experimental.pallas import tpu as pltpu
from jax.sharding import PartitionSpec as P

MESH = pl.DeviceIdType.MESH
F = 256
NI = 1024
SC = 256
K = 8
N = 16
SB = 16
ROUNDS = 4
CUTS = ((0, 0, 96, 96, 192, 256), (0, 96, 96, 192, 256), (0, 96, 96, 192, 256), (0, 96, 160, 208, 256))
OPP = (1, 0, 3, 2)
f32, bf16 = jnp.float32, jnp.bfloat16
NT = (((1,), (1,)), ((), ()))


def mm(a, b):
    return jnp.dot(a, b, preferred_element_type=f32)


def mm_nt(a, b):
    return lax.dot_general(a, b, NT, preferred_element_type=f32)


def split(x):
    hi = x.astype(bf16)
    return hi, (x - hi.astype(f32)).astype(bf16)


def split3(x):
    hi = x.astype(bf16)
    rest = x - hi.astype(f32)
    mid = rest.astype(bf16)
    return hi, mid, (rest - mid.astype(f32)).astype(bf16)


def kernel(
    schur_in, load_in, dscale_in, basis_in, cinv_in, north_in, west_in,
    sol_out, res_out,
    dscale, north, west,
    smat, shi, slo, y, us, r, p, s, x, uhi, ulo, dcol,
    pn, pw, bds, nbr_bds, bext, bst, gst, bcat, tcat, tau, sig,
    crow, chi, clo,
    halo, p1s, p1r, p1ns, p1nr, p2s, p2r, p3s, p3r, p3ns, p3nr, pm,
    local_sem, hs, hr, bs, br, cs, cr, s1, r1, s2, r2, s3, r3, out_sem,
):
    row, col = lax.axis_index("row"), lax.axis_index("col")
    has = (row > 0, row < N - 1, col > 0, col < N - 1)
    nbr = ((row - 1, col), (row + 1, col), (row, col - 1), (row, col + 1))
    wt = [jnp.where(h, 0.5, 1.0).astype(f32) for h in has]

    def fetch(i, src, dst):
        copy = pltpu.make_async_copy(src, dst, local_sem.at[i])
        copy.start()
        return copy

    get_small = [
        fetch(0, north_in, north), fetch(1, west_in, west), fetch(2, basis_in, bds.at[pl.ds(0, 8)]), fetch(3, dscale_in, dscale),
    ]
    get_cinv = fetch(4, cinv_in, crow.at[col])
    get_load = fetch(5, load_in, y)
    get_s = fetch(6, schur_in, smat)

    barrier = pltpu.get_barrier_semaphore()

    def greet(i, _):
        pl.semaphore_signal(barrier, inc=1, device_id=(lax.rem(row + i, N), col), device_id_type=MESH)
        for step in (0, 1, N - 1):
            other = (lax.rem(row + step, N), lax.rem(col + i, N))
            pl.semaphore_signal(barrier, inc=1, device_id=other, device_id_type=MESH)
        return 0

    lax.fori_loop(1, N, greet, 0, unroll=True)

    for copy in get_small:
        copy.wait()

    slot = lax.broadcasted_iota(jnp.int32, (F, F), 0)
    pn[...] = jnp.where(slot == north[...], 1.0, 0.0).astype(bf16)
    pw[...] = jnp.where(slot == west[...], 1.0, 0.0).astype(bf16)

    for f in range(4):

        @pl.when(jnp.logical_not(has[f]))
        def _():
            nbr_bds[f] = jnp.zeros((16, F), f32)
            for rd in range(ROUNDS):
                halo[rd, f] = jnp.zeros((F, SC), f32)
            if f < 2:
                for rd in range(ROUNDS - 1):
                    p1nr[rd, f] = jnp.zeros((N, 1, 128), f32)
                    p3nr[rd, f] = jnp.zeros((N, 1, 128), f32)

    bds[8:16] = jnp.where(lax.broadcasted_iota(jnp.int32, (8, NI), 0) == 0, dscale[...], 0.0)
    for f, perm in ((0, pn), (2, pw)):
        parts = split3(bds[:, f * F : (f + 1) * F])
        hi, mid, lo = [mm_nt(part, perm[...]) for part in parts]
        bds[:, f * F : (f + 1) * F] = (hi + mid) + lo

    pl.semaphore_wait(barrier, 4 * (N - 1))

    def when_each(fn, faces=(0, 1, 2, 3)):
        for f in faces:
            pl.when(has[f])(functools.partial(fn, f))

    def face_basis(f):
        return pltpu.make_async_remote_copy(
            src_ref=bds.at[:, pl.ds(f * F, F)], dst_ref=nbr_bds.at[OPP[f]], send_sem=bs.at[f], recv_sem=br.at[OPP[f]],
            device_id=nbr[f], device_id_type=MESH,
        )

    when_each(lambda f: face_basis(f).start())

    def copy_to(src, dst, send_sem, recv_sem, dev):
        return pltpu.make_async_remote_copy(
            src_ref=src, dst_ref=dst, send_sem=send_sem, recv_sem=recv_sem, device_id=dev, device_id_type=MESH
        )

    def along_col(first, up, src_of, dst, send_sem, recv_sem):
        def send(i, _):
            to = lax.rem(col + i, N)
            copy_to(src_of(to), dst, send_sem, recv_sem, (row - up, to)).start()
            return 0

        lax.fori_loop(first, N, send, 0, unroll=True)

    def three_rows(up_src, down_src, up_dst, down_dst, src_of, dst, send_sem, recv_sem):
        pl.when(has[0])(lambda: along_col(0, 1, lambda to: up_src.at[to], up_dst.at[col], send_sem.at[1], recv_sem.at[2]))
        pl.when(has[1])(lambda: along_col(0, -1, lambda to: down_src.at[to], down_dst.at[col], send_sem.at[2], recv_sem.at[1]))
        along_col(1, 0, src_of, dst, send_sem.at[0], recv_sem.at[0])

    def along_row(src, dst, send_sem, recv_sem):
        def send(i, _):
            copy_to(src, dst, send_sem, recv_sem, (lax.rem(row + i, N), col)).start()
            return 0

        lax.fori_loop(1, N, send, 0, unroll=True)

    def wait_many(buf, sem, count=N - 1):
        part = buf.at[pl.ds(0, count)]
        pltpu.make_async_copy(part, part, sem).wait()

    def three_waits(own, other, sem, between=None):
        wait_many(own, sem.at[0])
        if between is not None:
            between()
        for f in (0, 1):
            pl.when(has[f])(functools.partial(wait_many, other.at[f], sem.at[f + 1], N))

    get_cinv.wait()
    mine = crow.at[col]

    def send_cinv(i, _):
        copy_to(mine, mine, cs.at[0], cr.at[0], (row, lax.rem(col + 2 * i, N))).start()
        return 0

    lax.fori_loop(1, N // 2, send_cinv, 0)
    partner = col + 1 - 2 * lax.rem(col, 2)

    def pass_cinv():
        wait_many(crow, cr.at[0], N // 2 - 1)

        def send(i, _):
            block = crow.at[2 * i + lax.rem(col, 2)]
            copy_to(block, block, cs.at[1], cr.at[1], (row, partner)).start()
            return 0

        lax.fori_loop(0, N // 2, send, 0)

    def chunk(rd, q, faces=(0, 1, 2, 3)):
        cuts = CUTS[rd]
        start, rows = cuts[q], cuts[q + 1] - cuts[q]
        if rows == 0:
            return

        def one(f):
            pltpu.make_async_remote_copy(
                src_ref=y.at[pl.ds(f * F + start, rows)], dst_ref=halo.at[rd, OPP[f], pl.ds(start, rows)],
                send_sem=hs.at[rd, f], recv_sem=hr.at[rd, OPP[f]], device_id=nbr[f], device_id_type=MESH,
            ).start()

        when_each(one, faces)

    def halo_sent(rd):
        def one(f):
            part = y.at[pl.ds(f * F, F)]
            pltpu.make_async_copy(part, part, hs.at[rd, f]).wait()

        when_each(one)

    def halo_wait(rd, f):
        @pl.when(has[f])
        def _():
            part = halo.at[rd, f]
            pltpu.make_async_copy(part, part, hr.at[rd, f]).wait()

    get_load.wait()
    for f, perm in ((0, pn), (2, pw)):
        parts = split3(y[f * F : (f + 1) * F, :])
        hi, mid, lo = [mm(perm[...], part) for part in parts]
        y[f * F : (f + 1) * F, :] = (hi + mid) + lo
    vhi, vlo = split(y[...])
    uhi[...] = vhi
    ulo[...] = vlo

    chunk(0, 0)

    def wait_basis(f):
        part = nbr_bds.at[f]
        pltpu.make_async_copy(part, part, br.at[f]).wait()

    when_each(wait_basis)
    bext[...] = jnp.zeros_like(bext)
    drow = []
    for f in range(4):
        at = slice(f * F, (f + 1) * F)
        bext[0:8, at] = wt[f] * bds[0:8, at]
        bext[8 + 8 * f : 16 + 8 * f, at] = wt[f] * nbr_bds[f, 0:8]
        drow.append((wt[f] * wt[f]) * (bds[8:9, at] + nbr_bds[f, 8:9]))
    bhi, blo = split(bext[...])
    bst[0:48] = bhi
    bst[48:96] = blo

    lane = lax.broadcasted_iota(jnp.int32, (8, 128), 1)
    lane_group = lax.shift_right_logical(lane, 4)
    sub = lax.broadcasted_iota(jnp.int32, (8, 128), 0)
    lane_group16 = lax.shift_right_logical(lax.broadcasted_iota(jnp.int32, (SB, 128), 1), 4)
    diagonal = jnp.bitwise_and(lane_group - sub, 7)

    def turn(tile):
        out = tile
        for d in range(1, 8):
            out = jnp.where(diagonal == d, pltpu.roll(pltpu.roll(tile, SB * d, 1), 8 - d, 0), out)
        return out

    def to_blocks(part):
        return jnp.concatenate([turn(part[:, 0:128]), turn(part[:, 128:256])], axis=0)

    def from_blocks(part):
        return jnp.concatenate([turn(part[0:8]), turn(part[8:16])], axis=1)

    def rows_tile(rows):
        tile = jnp.zeros((8, 128), f32)
        for i, v in enumerate(rows):
            tile = jnp.where(sub == i, v, tile)
        return tile


    def contributions(rd, mat):
        both = mm(mat[...], uhi[...])
        c48 = both[0:48] + (both[48:96] + mm(mat[0:48], ulo[...]))
        own, north_part, south_part, west_part, east_part = [to_blocks(c48[8 * g : 8 * g + 8]) for g in range(5)]
        p1ns[rd, 0] = north_part.reshape(N, 1, 128)
        p1ns[rd, 1] = south_part.reshape(N, 1, 128)
        for b in range(N):
            p1s[rd, b] = rows_tile([part[b : b + 1] for part in (own, west_part, east_part)])
        p1r[rd, col] = p1s[rd, col]
        three_rows(
            p1ns.at[rd, 0], p1ns.at[rd, 1], p1nr.at[rd, 1], p1nr.at[rd, 0], lambda to: p1s.at[rd, to], p1r.at[rd, col],
            s1.at[rd], r1.at[rd],
        )

    def up_one(a):
        return jnp.concatenate([a[1:], a[:1]], axis=0)

    def down_one(a):
        return jnp.concatenate([a[N - 1 :], a[: N - 1]], axis=0)

    def gather_rows(rd, dots, between):
        three_waits(p1r.at[rd], p1nr.at[rd], r1.at[rd], between)
        own, west_part, east_part = [
            jnp.concatenate([p1r[rd, i, g : g + 1] for i in range(N)], axis=0) for g in range(3)
        ]
        block = (own + (p1nr[rd, 0].reshape(N, 128) + p1nr[rd, 1].reshape(N, 128))) + (up_one(west_part) + down_one(east_part))
        turned = jnp.concatenate([block, jnp.zeros((128 - N, 128), f32)], axis=0).T
        rhs = turned[0:SB]
        for k in range(1, K):
            rhs = jnp.where(lane_group16 == k, pltpu.roll(turned[SB * k : SB * k + SB], SB * k, 1), rhs)
        p2s[rd, 0:SB] = rhs
        p2s[rd, SB : SB + 8] = dots
        p2r[rd, row] = p2s[rd]
        along_row(p2s.at[rd], p2r.at[rd, row], s2.at[rd], r2.at[rd])

    def sum_tiles(buf, at):
        total = buf[0, at : at + 8]
        for i in range(1, N):
            total = total + buf[i, at : at + 8]
        return total

    def solve(rd):
        wait_many(p2r.at[rd], r2.at[rd])
        rhs = jnp.concatenate([p2r[rd, i, 0:SB] for i in range(N)], axis=1)
        hi, lo = split(rhs)
        both = mm_nt(jnp.concatenate([hi, lo], axis=0), chi[...])
        solved = both[0:SB] + (both[SB : 2 * SB] + mm_nt(hi, clo[...]))
        pieces = [solved] + [pltpu.roll(solved, 128 - SB * k, 1) for k in range(1, K)]
        own = jnp.concatenate(pieces, axis=0).T[0:N]
        east_of, west_of = up_one(own), down_one(own)
        dots = sum_tiles(p2r.at[rd], SB)
        p3ns[rd] = own.reshape(N, 1, 128)
        for i in range(N):
            p3s[rd, i, 0:8] = rows_tile([part[i : i + 1] for part in (own, west_of, east_of)])
            p3s[rd, i, 8:16] = dots
        p3r[rd, col] = p3s[rd, col]
        three_rows(
            p3ns.at[rd], p3ns.at[rd], p3nr.at[rd, 1], p3nr.at[rd, 0], lambda to: p3s.at[rd, to], p3r.at[rd, col],
            s3.at[rd], r3.at[rd],
        )

    def solutions(rd):
        three_waits(p3r.at[rd], p3nr.at[rd], r3.at[rd])
        own, west_of, east_of = [jnp.concatenate([p3r[rd, i, g : g + 1] for i in range(N)], axis=0) for g in range(3)]
        parts = [own, p3nr[rd, 0].reshape(N, 128), p3nr[rd, 1].reshape(N, 128), west_of, east_of]
        return jnp.concatenate([from_blocks(part) for part in parts], axis=0), sum_tiles(p3r.at[rd], 8)

    def set_tau(new):
        tau[...] = new
        hi = new.astype(bf16).astype(f32)
        tcat[0:40] = hi.astype(bf16)
        tcat[64:104] = (new - hi).astype(bf16)
        tcat[128:168] = hi.astype(bf16)

    def dot_tile(delta, gamma, eps):
        tile = jnp.zeros((8, 128), f32)
        for i, v in enumerate((delta, gamma, eps)):
            if v is not None:
                tile = jnp.where(sub == 2 * i, v[:, 0:128], tile)
                tile = jnp.where(sub == 2 * i + 1, v[:, 128:256], tile)
        return tile

    def scalars(tile):
        return [jnp.concatenate([tile[2 * i : 2 * i + 1], tile[2 * i + 1 : 2 * i + 2]], axis=1) for i in range(3)]

    def prepare_rows(f):
        at = slice(f * F, (f + 1) * F)
        parts = list(split(smat[at, :]))
        for part, dst in zip(parts, (shi, slo)):
            if f == 0:
                part = mm(pn[...], part).astype(bf16)
            elif f == 2:
                part = mm(pw[...], part).astype(bf16)
            dst[at, 0:F] = mm_nt(part[:, 0:F], pn[...]).astype(bf16)
            dst[at, F : 2 * F] = part[:, F : 2 * F]
            dst[at, 2 * F : 3 * F] = mm_nt(part[:, 2 * F : 3 * F], pw[...]).astype(bf16)
            dst[at, 3 * F :] = part[:, 3 * F :]

    def new_u(rd, f):
        at = slice(f * F, (f + 1) * F)
        d = dcol[at, :]
        res = r[at, :]
        val = jnp.concatenate([d, d], axis=1) * res + mm(bcat[at, :], tcat[...])
        us[(rd + 1) % 2, at, :] = val
        hi, lo = split(val)
        uhi[at, :] = hi
        ulo[at, :] = lo
        return wt[f] * jnp.sum(res * val, axis=0, keepdims=True), val

    def own_order(f, val):
        if f in (1, 3):
            return val
        perm = (pn if f == 0 else pw)[...]
        hi, mid, lo = [
            lax.dot_general(perm, part, (((0,), (0,)), ((), ())), preferred_element_type=f32) for part in split3(val)
        ]
        return (hi + mid) + lo

    def apply_schur(rd, after_face):
        total = jnp.zeros((1, SC), f32)
        for f in range(4):
            at = slice(f * F, (f + 1) * F)
            val = mm(shi[at, :], uhi[...]) + (mm(shi[at, :], ulo[...]) + mm(slo[at, :], uhi[...]))
            y[at, :] = val
            after_face(f)
            total = total + jnp.sum(us[rd % 2, at, :] * val, axis=0, keepdims=True)
        return total

    def move(rd, alpha, beta, write):
        for f in range(4):
            at = slice(f * F, (f + 1) * F)
            direction = us[rd % 2, at, :]
            if beta is not None:
                direction = direction + beta * p[at, :]
            iterate = alpha * direction
            if beta is not None:
                iterate = iterate + x[at, :]
            if write is None:
                p[at, :] = direction
                x[at, :] = iterate
            else:
                write(f, iterate)

    contributions(0, bst)
    chunk(0, 1)
    get_s.wait()
    prepare_rows(0)
    prepare_rows(1)
    gather_rows(0, jnp.zeros((8, 128), f32), lambda: chunk(0, 2))
    pass_cinv()
    chunk(0, 3)
    prepare_rows(2)
    prepare_rows(3)
    wait_many(crow, cr.at[1], N // 2)
    order = lax.broadcasted_iota(jnp.int32, (128, 128), 0)
    order = jnp.bitwise_and(order, N - 1) * K + lax.shift_right_logical(order, 4)
    pm[...] = jnp.where(order == lax.broadcasted_iota(jnp.int32, (128, 128), 1), 1.0, 0.0).astype(bf16)
    for part, dst in zip(split(crow[...].reshape(128, N * 128)), (chi, clo)):
        part = mm(pm[...], part).astype(bf16)
        for i in range(N):
            dst[:, i * 128 : i * 128 + 128] = mm_nt(part[:, i * 128 : i * 128 + 128], pm[...]).astype(bf16)
    solve(0)
    chunk(0, 4)
    both = mm(bst[...], shi[...])
    gt = both[0:48] + (both[48:96] + mm(bst[0:48], slo[...]))
    ghi, glo = split(gt)
    gst[0:48] = ghi
    gst[48:96] = glo
    tcat[...] = jnp.zeros_like(tcat)
    bhi32 = bext[...].astype(bf16).astype(f32)
    blo32 = bext[...] - bhi32
    pad = jnp.zeros((16, NI), f32)
    bcat[...] = jnp.concatenate([bhi32, pad, bhi32, pad, blo32, pad, jnp.zeros((64, NI), f32)], axis=0).T.astype(bf16)
    dcol[...] = jnp.broadcast_to(jnp.concatenate(drow, axis=1), (128, NI)).T
    set_tau(solutions(0)[0])
    gamma = jnp.zeros((1, SC), f32)
    for f in (3, 2, 1, 0):
        at = slice(f * F, (f + 1) * F)
        halo_wait(0, f)
        r[at, :] = y[at, :] + halo[0, f]
        gamma = gamma + new_u(0, f)[0]
    halo_sent(0)

    eps = None
    gamma_old = pap_old = pending = None
    for rd in range(1, ROUNDS):
        last = rd == ROUNDS - 1
        if not last:
            contributions(rd, gst)
        delta = apply_schur(rd, (lambda f: None) if last else (lambda f: chunk(rd, 0, (f,))))
        dots = dot_tile(delta, gamma, eps)
        if not last:
            if pending is not None:
                move(*pending, None)
            gather_rows(rd, dots, lambda: chunk(rd, 1))
            chunk(rd, 2)
            solve(rd)
            chunk(rd, 3)
            solved, total = solutions(rd)
        else:
            p2s[rd, SB : SB + 8] = dots
            p2r[rd, row, SB : SB + 8] = dots
            along_row(p2s.at[rd, pl.ds(SB, 8)], p2r.at[rd, row, pl.ds(SB, 8)], s2.at[rd], r2.at[rd])
            chunk(rd, 0)
            chunk(rd, 1)
            chunk(rd, 2)
            move(*pending, None)
            wait_many(p2r.at[rd, :, pl.ds(SB, 8)], r2.at[rd])
            dots = sum_tiles(p2r.at[rd], SB)
            p3s[rd, 0, 8:16] = dots
            p3r[rd, col, 8:16] = dots
            along_col(1, 0, lambda to: p3s.at[rd, 0, pl.ds(8, 8)], p3r.at[rd, col, pl.ds(8, 8)], s3.at[rd, 0], r3.at[rd, 0])
            chunk(rd, 3)
            wait_many(p3r.at[rd, :, pl.ds(8, 8)], r3.at[rd, 0])
            total = sum_tiles(p3r.at[rd], 8)
        delta_t, gamma_t, eps_t = scalars(total)
        if rd == 1:
            beta = None
            pap = delta_t
        else:
            beta = gamma_t / gamma_old
            pap = delta_t + beta * (2.0 * eps_t + beta * pap_old)
        alpha = gamma_t / pap
        gamma_old, pap_old = gamma_t, pap
        if not last:
            if beta is not None:
                solved = solved + beta * sig[...]
            sig[...] = solved
            set_tau(tau[...] - alpha * solved)
        if last:

            def write(f, val):
                x[f * F : (f + 1) * F, :] = own_order(f, val)
                pltpu.make_async_copy(x.at[pl.ds(f * F, F)], sol_out.at[pl.ds(f * F, F)], out_sem.at[0]).start()

            move(rd, alpha, beta, write)
        pending = (rd, alpha, beta)
        gamma = jnp.zeros((1, SC), f32)
        eps = jnp.zeros((1, SC), f32)
        for f in (3, 2, 1, 0):
            at = slice(f * F, (f + 1) * F)
            halo_wait(rd, f)
            image = y[at, :] + halo[rd, f]
            if beta is not None:
                image = image + beta * s[at, :]
            res = r[at, :] - alpha * image
            if last:
                r[at, :] = own_order(f, res)
                pltpu.make_async_copy(r.at[pl.ds(f * F, F)], res_out.at[pl.ds(f * F, F)], out_sem.at[1]).start()
            else:
                r[at, :] = res
                s[at, :] = image
                share, val = new_u(rd, f)
                gamma = gamma + share
                eps = eps + wt[f] * jnp.sum(val * image, axis=0, keepdims=True)
        halo_sent(rd)

    pltpu.make_async_copy(x, sol_out, out_sem.at[0]).wait()
    pltpu.make_async_copy(r, res_out, out_sem.at[1]).wait()
    when_each(lambda f: face_basis(f).wait_send())
    wait_many(crow, cs.at[0], N // 2 - 1)
    wait_many(crow, cs.at[1], N // 2)
    for rd in range(ROUNDS):
        if rd < ROUNDS - 1:
            three_waits(p1r.at[rd], p1nr.at[rd], s1.at[rd])
            wait_many(p2r.at[rd], s2.at[rd])
            three_waits(p3r.at[rd], p3nr.at[rd], s3.at[rd])
        else:
            wait_many(p2r.at[rd, :, pl.ds(SB, 8)], s2.at[rd])
            wait_many(p3r.at[rd, :, pl.ds(8, 8)], s3.at[rd, 0])


def body(schur, load, dscale, basis, coarse_inv, north_match, west_match):
    vmem = pl.BlockSpec(memory_space=pltpu.VMEM)
    hbm = pl.BlockSpec(memory_space=pltpu.HBM)
    dma = pltpu.SemaphoreType.DMA

    def buf(*shape, dtype=f32):
        return pltpu.VMEM(shape, dtype)

    vec = buf(NI, SC)
    half = buf(NI, SC, dtype=bf16)
    solved, left = pl.pallas_call(
        kernel,
        out_shape=[jax.ShapeDtypeStruct((NI, SC), f32)] * 2,
        in_specs=[hbm] * 7,
        out_specs=[hbm, hbm],
        scratch_shapes=[
            buf(1, NI), buf(1, F, dtype=jnp.int32), buf(1, F, dtype=jnp.int32),
            buf(NI, NI), buf(NI, NI, dtype=bf16), buf(NI, NI, dtype=bf16),
            vec, buf(2, NI, SC), vec, vec, vec, vec, half, half, buf(NI, 128),
            buf(F, F, dtype=bf16), buf(F, F, dtype=bf16), buf(16, NI), buf(4, 16, F), buf(48, NI),
            buf(96, NI, dtype=bf16), buf(96, NI, dtype=bf16), buf(NI, 256, dtype=bf16), buf(256, SC, dtype=bf16),
            buf(40, SC), buf(40, SC),
            buf(N, K, N * 128), buf(128, N * 128, dtype=bf16), buf(128, N * 128, dtype=bf16),
            buf(ROUNDS, 4, F, SC),
            buf(ROUNDS, N, 8, 128), buf(ROUNDS, N, 8, 128), buf(ROUNDS, 2, N, 1, 128), buf(ROUNDS, 2, N, 1, 128),
            buf(ROUNDS, SB + 8, 128), buf(ROUNDS, N, SB + 8, 128),
            buf(ROUNDS, N, 16, 128), buf(ROUNDS, N, 16, 128), buf(ROUNDS, N, 1, 128), buf(ROUNDS, 2, N, 1, 128),
            buf(128, 128, dtype=bf16),
            dma((7,)), dma((ROUNDS, 4)), dma((ROUNDS, 4)), dma((4,)), dma((4,)), dma((2,)), dma((2,)),
            dma((ROUNDS, 3)), dma((ROUNDS, 3)), dma((ROUNDS,)), dma((ROUNDS,)), dma((ROUNDS, 3)), dma((ROUNDS, 3)), dma((2,)),
        ],
        compiler_params=pltpu.CompilerParams(collective_id=0, has_side_effects=True, vmem_limit_bytes=63 << 20),
    )(
        schur.reshape(NI, NI), load.reshape(NI, SC), dscale.reshape(1, NI), basis.reshape(K, NI),
        coarse_inv, north_match.reshape(1, F), west_match.reshape(1, F),
    )
    return solved.reshape(1, 1, NI, SC), left.reshape(1, 1, NI, SC)


def solution(mesh):
    placed = (
        P("row", "col", None, None),
        P("row", "col", None, None),
        P("row", "col", None),
        P("row", "col", None, None),
        P(("row", "col"), None),
        P("row", "col", None),
        P("row", "col", None),
    )
    return jax.shard_map(
        body,
        mesh=mesh,
        in_specs=placed,
        out_specs=(P("row", "col", None, None), P("row", "col", None, None)),
        check_vma=False,
    )
```

```python
import functools

import jax
import jax.numpy as jnp
from jax import lax
from jax.experimental import pallas as pl
from jax.experimental.pallas import tpu as pltpu
from jax.sharding import PartitionSpec as P

MESH = pl.DeviceIdType.MESH
F = 256
NI = 1024
SC = 256
K = 8
N = 16
SB = 16
ROUNDS = 4
CUTS = ((0, 0, 96, 96, 192, 256), (0, 96, 96, 192, 256), (0, 96, 96, 192, 256), (0, 96, 160, 208, 256))
PIECES = 4
OPP = (1, 0, 3, 2)
f32, bf16 = jnp.float32, jnp.bfloat16
NT = (((1,), (1,)), ((), ()))


def mm(a, b):
    return jnp.dot(a, b, preferred_element_type=f32)


def mm_nt(a, b):
    return lax.dot_general(a, b, NT, preferred_element_type=f32)


def split(x):
    hi = x.astype(bf16)
    return hi, (x - hi.astype(f32)).astype(bf16)


def split3(x):
    hi = x.astype(bf16)
    rest = x - hi.astype(f32)
    mid = rest.astype(bf16)
    return hi, mid, (rest - mid.astype(f32)).astype(bf16)


def kernel(
    schur_in, load_in, dscale_in, basis_in, cinv_in, north_in, west_in,
    sol_out, res_out,
    dscale, north, west,
    smat, shi, slo, y, us, r, p, s, x, uhi, ulo, dcol,
    pn, pw, bds, nbr_bds, bext, bst, gst, bcat, tcat, tau, sig,
    crow, chi, clo,
    halo, p1s, p1r, p1ns, p1nr, p2s, p2r, p3s, p3r, p3ns, p3nr, pm, d2s, d2r, d3s, d3r,
    local_sem, hs, hr, bs, br, cs, cr, s1, r1, s2, r2, s3, r3, out_sem, s4, r4, s5, r5,
):
    row, col = lax.axis_index("row"), lax.axis_index("col")
    has = (row > 0, row < N - 1, col > 0, col < N - 1)
    nbr = ((row - 1, col), (row + 1, col), (row, col - 1), (row, col + 1))
    wt = [jnp.where(h, 0.5, 1.0).astype(f32) for h in has]

    def fetch(i, src, dst):
        copy = pltpu.make_async_copy(src, dst, local_sem.at[i])
        copy.start()
        return copy

    get_small = [
        fetch(0, north_in, north), fetch(1, west_in, west), fetch(2, basis_in, bds.at[pl.ds(0, 8)]), fetch(3, dscale_in, dscale),
    ]
    get_cinv = fetch(4, cinv_in, crow.at[col])
    get_load = fetch(5, load_in, y)
    get_s = fetch(6, schur_in, smat)

    barrier = pltpu.get_barrier_semaphore()

    def greet(i, _):
        pl.semaphore_signal(barrier, inc=1, device_id=(lax.rem(row + i, N), col), device_id_type=MESH)
        for step in (0, 1, N - 1):
            other = (lax.rem(row + step, N), lax.rem(col + i, N))
            pl.semaphore_signal(barrier, inc=1, device_id=other, device_id_type=MESH)
        return 0

    lax.fori_loop(1, N, greet, 0, unroll=True)

    for copy in get_small:
        copy.wait()

    slot = lax.broadcasted_iota(jnp.int32, (F, F), 0)
    pn[...] = jnp.where(slot == north[...], 1.0, 0.0).astype(bf16)
    pw[...] = jnp.where(slot == west[...], 1.0, 0.0).astype(bf16)

    for f in range(4):

        @pl.when(jnp.logical_not(has[f]))
        def _():
            nbr_bds[f] = jnp.zeros((16, F), f32)
            for rd in range(ROUNDS):
                halo[rd, f] = jnp.zeros((F, SC), f32)
            if f < 2:
                for rd in range(ROUNDS - 1):
                    p1nr[rd, f] = jnp.zeros((N, 1, 128), f32)
                    p3nr[rd, f] = jnp.zeros((N, 1, 128), f32)

    bds[8:16] = jnp.where(lax.broadcasted_iota(jnp.int32, (8, NI), 0) == 0, dscale[...], 0.0)
    for f, perm in ((0, pn), (2, pw)):
        parts = split3(bds[:, f * F : (f + 1) * F])
        hi, mid, lo = [mm_nt(part, perm[...]) for part in parts]
        bds[:, f * F : (f + 1) * F] = (hi + mid) + lo

    pl.semaphore_wait(barrier, 4 * (N - 1))

    def when_each(fn, faces=(0, 1, 2, 3)):
        for f in faces:
            pl.when(has[f])(functools.partial(fn, f))

    def face_basis(f):
        return pltpu.make_async_remote_copy(
            src_ref=bds.at[:, pl.ds(f * F, F)], dst_ref=nbr_bds.at[OPP[f]], send_sem=bs.at[f], recv_sem=br.at[OPP[f]],
            device_id=nbr[f], device_id_type=MESH,
        )

    when_each(lambda f: face_basis(f).start())

    def copy_to(src, dst, send_sem, recv_sem, dev):
        return pltpu.make_async_remote_copy(
            src_ref=src, dst_ref=dst, send_sem=send_sem, recv_sem=recv_sem, device_id=dev, device_id_type=MESH
        )

    def along_col(first, up, src_of, dst, send_sem, recv_sem):
        def send(i, _):
            to = lax.rem(col + i, N)
            copy_to(src_of(to), dst, send_sem, recv_sem, (row - up, to)).start()
            return 0

        lax.fori_loop(first, N, send, 0, unroll=True)

    def three_rows(up_src, down_src, up_dst, down_dst, src_of, dst, send_sem, recv_sem):
        pl.when(has[0])(lambda: along_col(0, 1, lambda to: up_src.at[to], up_dst.at[col], send_sem.at[1], recv_sem.at[2]))
        pl.when(has[1])(lambda: along_col(0, -1, lambda to: down_src.at[to], down_dst.at[col], send_sem.at[2], recv_sem.at[1]))
        along_col(1, 0, src_of, dst, send_sem.at[0], recv_sem.at[0])

    def along_row(src, dst, send_sem, recv_sem):
        def send(i, _):
            copy_to(src, dst, send_sem, recv_sem, (lax.rem(row + i, N), col)).start()
            return 0

        lax.fori_loop(1, N, send, 0, unroll=True)

    def wait_many(buf, sem, count=N - 1):
        part = buf.at[pl.ds(0, count)]
        pltpu.make_async_copy(part, part, sem).wait()

    def three_waits(own, other, sem, between=None):
        wait_many(own, sem.at[0])
        if between is not None:
            between()
        for f in (0, 1):
            pl.when(has[f])(functools.partial(wait_many, other.at[f], sem.at[f + 1], N))

    get_cinv.wait()
    mine = crow.at[col]

    def send_cinv(i, _):
        copy_to(mine, mine, cs.at[0], cr.at[0], (row, lax.rem(col + 2 * i, N))).start()
        return 0

    lax.fori_loop(1, N // 2, send_cinv, 0)
    partner = col + 1 - 2 * lax.rem(col, 2)

    def pass_cinv():
        wait_many(crow, cr.at[0], N // 2 - 1)

        def send(i, _):
            block = crow.at[2 * i + lax.rem(col, 2)]
            copy_to(block, block, cs.at[1], cr.at[1], (row, partner)).start()
            return 0

        lax.fori_loop(0, N // 2, send, 0)

    def chunk(rd, q, faces=(0, 1, 2, 3)):
        cuts = CUTS[rd]
        start, rows = cuts[q], cuts[q + 1] - cuts[q]
        if rows == 0:
            return

        def one(f):
            pltpu.make_async_remote_copy(
                src_ref=y.at[pl.ds(f * F + start, rows)], dst_ref=halo.at[rd, OPP[f], pl.ds(start, rows)],
                send_sem=hs.at[rd, f], recv_sem=hr.at[rd, OPP[f]], device_id=nbr[f], device_id_type=MESH,
            ).start()

        when_each(one, faces)

    def halo_sent(rd):
        def one(f):
            part = y.at[pl.ds(f * F, F)]
            pltpu.make_async_copy(part, part, hs.at[rd, f]).wait()

        when_each(one)

    def halo_wait(rd, f):
        @pl.when(has[f])
        def _():
            part = halo.at[rd, f]
            pltpu.make_async_copy(part, part, hr.at[rd, f]).wait()

    get_load.wait()
    for f, perm in ((0, pn), (2, pw)):
        parts = split3(y[f * F : (f + 1) * F, :])
        hi, mid, lo = [mm(perm[...], part) for part in parts]
        y[f * F : (f + 1) * F, :] = (hi + mid) + lo
    vhi, vlo = split(y[...])
    uhi[...] = vhi
    ulo[...] = vlo

    chunk(0, 0)

    def wait_basis(f):
        part = nbr_bds.at[f]
        pltpu.make_async_copy(part, part, br.at[f]).wait()

    when_each(wait_basis)
    bext[...] = jnp.zeros_like(bext)
    drow = []
    for f in range(4):
        at = slice(f * F, (f + 1) * F)
        bext[0:8, at] = wt[f] * bds[0:8, at]
        bext[8 + 8 * f : 16 + 8 * f, at] = wt[f] * nbr_bds[f, 0:8]
        drow.append((wt[f] * wt[f]) * (bds[8:9, at] + nbr_bds[f, 8:9]))
    bhi, blo = split(bext[...])
    bst[0:48] = bhi
    bst[48:96] = blo

    lane = lax.broadcasted_iota(jnp.int32, (8, 128), 1)
    lane_group = lax.shift_right_logical(lane, 4)
    sub = lax.broadcasted_iota(jnp.int32, (8, 128), 0)
    lane_group16 = lax.shift_right_logical(lax.broadcasted_iota(jnp.int32, (SB, 128), 1), 4)
    diagonal = jnp.bitwise_and(lane_group - sub, 7)

    def turn(tile):
        out = tile
        for d in range(1, 8):
            out = jnp.where(diagonal == d, pltpu.roll(pltpu.roll(tile, SB * d, 1), 8 - d, 0), out)
        return out

    def to_blocks(part):
        return jnp.concatenate([turn(part[:, 0:128]), turn(part[:, 128:256])], axis=0)

    def from_blocks(part):
        return jnp.concatenate([turn(part[0:8]), turn(part[8:16])], axis=1)

    def rows_tile(rows):
        tile = jnp.zeros((8, 128), f32)
        for i, v in enumerate(rows):
            tile = jnp.where(sub == i, v, tile)
        return tile


    def contributions(rd, mat):
        both = mm(mat[...], uhi[...])
        c48 = both[0:48] + (both[48:96] + mm(mat[0:48], ulo[...]))
        own, north_part, south_part, west_part, east_part = [to_blocks(c48[8 * g : 8 * g + 8]) for g in range(5)]
        p1ns[rd, 0] = north_part.reshape(N, 1, 128)
        p1ns[rd, 1] = south_part.reshape(N, 1, 128)
        for b in range(N):
            p1s[rd, b] = rows_tile([part[b : b + 1] for part in (own, west_part, east_part)])
        p1r[rd, col] = p1s[rd, col]
        three_rows(
            p1ns.at[rd, 0], p1ns.at[rd, 1], p1nr.at[rd, 1], p1nr.at[rd, 0], lambda to: p1s.at[rd, to], p1r.at[rd, col],
            s1.at[rd], r1.at[rd],
        )

    def up_one(a):
        return jnp.concatenate([a[1:], a[:1]], axis=0)

    def down_one(a):
        return jnp.concatenate([a[N - 1 :], a[: N - 1]], axis=0)

    def gather_rows(rd, between):
        three_waits(p1r.at[rd], p1nr.at[rd], r1.at[rd], between)
        own, west_part, east_part = [
            jnp.concatenate([p1r[rd, i, g : g + 1] for i in range(N)], axis=0) for g in range(3)
        ]
        block = (own + (p1nr[rd, 0].reshape(N, 128) + p1nr[rd, 1].reshape(N, 128))) + (up_one(west_part) + down_one(east_part))
        turned = jnp.concatenate([block, jnp.zeros((128 - N, 128), f32)], axis=0).T
        rhs = turned[0:SB]
        for k in range(1, K):
            rhs = jnp.where(lane_group16 == k, pltpu.roll(turned[SB * k : SB * k + SB], SB * k, 1), rhs)
        p2s[rd] = rhs
        p2r[rd, row] = p2s[rd]
        along_row(p2s.at[rd], p2r.at[rd, row], s2.at[rd], r2.at[rd])

    def sum_tiles(buf):
        total = buf[0]
        for i in range(1, N):
            total = total + buf[i]
        return total

    def dots_row(rd, dots):
        d2s[rd] = dots
        d2r[rd, row] = dots
        along_row(d2s.at[rd], d2r.at[rd, row], s4.at[rd], r4.at[rd])

    def dots_col(rd):
        wait_many(d2r.at[rd], r4.at[rd])
        dots = sum_tiles(d2r.at[rd])
        d3s[rd] = dots
        d3r[rd, col] = dots
        along_col(1, 0, lambda to: d3s.at[rd], d3r.at[rd, col], s5.at[rd], r5.at[rd])

    def dots_total(rd):
        wait_many(d3r.at[rd], r5.at[rd])
        return sum_tiles(d3r.at[rd])

    def solve(rd):
        wait_many(p2r.at[rd], r2.at[rd])
        rhs = jnp.concatenate([p2r[rd, i] for i in range(N)], axis=1)
        hi, lo = split(rhs)
        both = mm_nt(jnp.concatenate([hi, lo], axis=0), chi[...])
        solved = both[0:SB] + (both[SB : 2 * SB] + mm_nt(hi, clo[...]))
        pieces = [solved] + [pltpu.roll(solved, 128 - SB * k, 1) for k in range(1, K)]
        own = jnp.concatenate(pieces, axis=0).T[0:N]
        east_of, west_of = up_one(own), down_one(own)
        p3ns[rd] = own.reshape(N, 1, 128)
        for i in range(N):
            p3s[rd, i] = rows_tile([part[i : i + 1] for part in (own, west_of, east_of)])
        p3r[rd, col] = p3s[rd, col]
        three_rows(
            p3ns.at[rd], p3ns.at[rd], p3nr.at[rd, 1], p3nr.at[rd, 0], lambda to: p3s.at[rd, to], p3r.at[rd, col],
            s3.at[rd], r3.at[rd],
        )

    def solutions(rd):
        three_waits(p3r.at[rd], p3nr.at[rd], r3.at[rd])
        own, west_of, east_of = [jnp.concatenate([p3r[rd, i, g : g + 1] for i in range(N)], axis=0) for g in range(3)]
        parts = [own, p3nr[rd, 0].reshape(N, 128), p3nr[rd, 1].reshape(N, 128), west_of, east_of]
        return jnp.concatenate([from_blocks(part) for part in parts], axis=0)

    def set_tau(new):
        tau[...] = new
        hi = new.astype(bf16).astype(f32)
        tcat[0:40] = hi.astype(bf16)
        tcat[64:104] = (new - hi).astype(bf16)
        tcat[128:168] = hi.astype(bf16)

    def dot_tile(delta, gamma, eps):
        tile = jnp.zeros((8, 128), f32)
        for i, v in enumerate((delta, gamma, eps)):
            if v is not None:
                tile = jnp.where(sub == 2 * i, v[:, 0:128], tile)
                tile = jnp.where(sub == 2 * i + 1, v[:, 128:256], tile)
        return tile

    def scalars(tile):
        return [jnp.concatenate([tile[2 * i : 2 * i + 1], tile[2 * i + 1 : 2 * i + 2]], axis=1) for i in range(3)]

    def prepare_rows(f):
        at = slice(f * F, (f + 1) * F)
        parts = list(split(smat[at, :]))
        for part, dst in zip(parts, (shi, slo)):
            if f == 0:
                part = mm(pn[...], part).astype(bf16)
            elif f == 2:
                part = mm(pw[...], part).astype(bf16)
            dst[at, 0:F] = mm_nt(part[:, 0:F], pn[...]).astype(bf16)
            dst[at, F : 2 * F] = part[:, F : 2 * F]
            dst[at, 2 * F : 3 * F] = mm_nt(part[:, 2 * F : 3 * F], pw[...]).astype(bf16)
            dst[at, 3 * F :] = part[:, 3 * F :]

    def new_u(rd, f):
        at = slice(f * F, (f + 1) * F)
        d = dcol[at, :]
        res = r[at, :]
        val = jnp.concatenate([d, d], axis=1) * res + mm(bcat[at, :], tcat[...])
        us[(rd + 1) % 2, at, :] = val
        hi, lo = split(val)
        uhi[at, :] = hi
        ulo[at, :] = lo
        return wt[f] * jnp.sum(res * val, axis=0, keepdims=True), val

    def own_order(f, val):
        if f in (1, 3):
            return val
        perm = (pn if f == 0 else pw)[...]
        hi, mid, lo = [
            lax.dot_general(perm, part, (((0,), (0,)), ((), ())), preferred_element_type=f32) for part in split3(val)
        ]
        return (hi + mid) + lo

    def apply_schur(rd, after_face):
        total = jnp.zeros((1, SC), f32)
        for f in range(4):
            at = slice(f * F, (f + 1) * F)
            val = mm(shi[at, :], uhi[...]) + (mm(shi[at, :], ulo[...]) + mm(slo[at, :], uhi[...]))
            y[at, :] = val
            after_face(f)
            total = total + jnp.sum(us[rd % 2, at, :] * val, axis=0, keepdims=True)
        return total

    def move(rd, alpha, beta, write):
        for f in range(4):
            at = slice(f * F, (f + 1) * F)
            direction = us[rd % 2, at, :]
            if beta is not None:
                direction = direction + beta * p[at, :]
            iterate = alpha * direction
            if beta is not None:
                iterate = iterate + x[at, :]
            if write is None:
                p[at, :] = direction
                x[at, :] = iterate
            else:
                write(f, iterate)

    contributions(0, bst)
    chunk(0, 1)
    get_s.wait()
    prepare_rows(0)
    prepare_rows(1)
    gather_rows(0, lambda: chunk(0, 2))
    pass_cinv()
    chunk(0, 3)
    prepare_rows(2)
    prepare_rows(3)
    wait_many(crow, cr.at[1], N // 2)
    order = lax.broadcasted_iota(jnp.int32, (128, 128), 0)
    order = jnp.bitwise_and(order, N - 1) * K + lax.shift_right_logical(order, 4)
    pm[...] = jnp.where(order == lax.broadcasted_iota(jnp.int32, (128, 128), 1), 1.0, 0.0).astype(bf16)
    for part, dst in zip(split(crow[...].reshape(128, N * 128)), (chi, clo)):
        part = mm(pm[...], part).astype(bf16)
        for i in range(N):
            dst[:, i * 128 : i * 128 + 128] = mm_nt(part[:, i * 128 : i * 128 + 128], pm[...]).astype(bf16)
    solve(0)
    chunk(0, 4)
    both = mm(bst[...], shi[...])
    gt = both[0:48] + (both[48:96] + mm(bst[0:48], slo[...]))
    ghi, glo = split(gt)
    gst[0:48] = ghi
    gst[48:96] = glo
    tcat[...] = jnp.zeros_like(tcat)
    bhi32 = bext[...].astype(bf16).astype(f32)
    blo32 = bext[...] - bhi32
    pad = jnp.zeros((16, NI), f32)
    bcat[...] = jnp.concatenate([bhi32, pad, bhi32, pad, blo32, pad, jnp.zeros((64, NI), f32)], axis=0).T.astype(bf16)
    dcol[...] = jnp.broadcast_to(jnp.concatenate(drow, axis=1), (128, NI)).T
    set_tau(solutions(0))
    gamma = jnp.zeros((1, SC), f32)
    for f in (3, 2, 1, 0):
        at = slice(f * F, (f + 1) * F)
        halo_wait(0, f)
        r[at, :] = y[at, :] + halo[0, f]
        gamma = gamma + new_u(0, f)[0]
    halo_sent(0)

    eps = None
    gamma_old = pap_old = pending = None
    for rd in range(1, ROUNDS):
        last = rd == ROUNDS - 1
        if not last:
            contributions(rd, gst)
        delta = apply_schur(rd, (lambda f: None) if last else (lambda f: chunk(rd, 0, (f,))))
        dots_row(rd, dot_tile(delta, gamma, eps))
        if not last:
            if pending is not None:
                move(*pending, None)
            gather_rows(rd, lambda: chunk(rd, 1))
            chunk(rd, 2)
            dots_col(rd)
            solve(rd)
            chunk(rd, 3)
            solved = solutions(rd)
        else:
            chunk(rd, 0)
            chunk(rd, 1)
            chunk(rd, 2)
            move(*pending, None)
            dots_col(rd)
            chunk(rd, 3)
        total = dots_total(rd)
        delta_t, gamma_t, eps_t = scalars(total)
        if rd == 1:
            beta = None
            pap = delta_t
        else:
            beta = gamma_t / gamma_old
            pap = delta_t + beta * (2.0 * eps_t + beta * pap_old)
        alpha = gamma_t / pap
        gamma_old, pap_old = gamma_t, pap
        if not last:
            if beta is not None:
                solved = solved + beta * sig[...]
            sig[...] = solved
            set_tau(tau[...] - alpha * solved)
        if last:

            def write(f, val):
                x[f * F : (f + 1) * F, :] = own_order(f, val)
                pltpu.make_async_copy(x.at[pl.ds(f * F, F)], sol_out.at[pl.ds(f * F, F)], out_sem.at[0]).start()

            move(rd, alpha, beta, write)
        pending = (rd, alpha, beta)
        gamma = jnp.zeros((1, SC), f32)
        eps = jnp.zeros((1, SC), f32)
        for f in (3, 2, 1, 0):
            at = slice(f * F, (f + 1) * F)
            halo_wait(rd, f)
            image = y[at, :] + halo[rd, f]
            if beta is not None:
                image = image + beta * s[at, :]
            res = r[at, :] - alpha * image
            if last:
                r[at, :] = own_order(f, res)
                pltpu.make_async_copy(r.at[pl.ds(f * F, F)], res_out.at[pl.ds(f * F, F)], out_sem.at[1]).start()
            else:
                r[at, :] = res
                s[at, :] = image
                share, val = new_u(rd, f)
                gamma = gamma + share
                eps = eps + wt[f] * jnp.sum(val * image, axis=0, keepdims=True)
        halo_sent(rd)

    pltpu.make_async_copy(x, sol_out, out_sem.at[0]).wait()
    pltpu.make_async_copy(r, res_out, out_sem.at[1]).wait()
    when_each(lambda f: face_basis(f).wait_send())
    wait_many(crow, cs.at[0], N // 2 - 1)
    wait_many(crow, cs.at[1], N // 2)
    for rd in range(ROUNDS):
        if rd < ROUNDS - 1:
            three_waits(p1r.at[rd], p1nr.at[rd], s1.at[rd])
            wait_many(p2r.at[rd], s2.at[rd])
            three_waits(p3r.at[rd], p3nr.at[rd], s3.at[rd])
        if rd > 0:
            wait_many(d2r.at[rd], s4.at[rd])
            wait_many(d3r.at[rd], s5.at[rd])


def deliver(a, b, a_out, b_out, a_mid, b_mid, in_sem, out_sem):
    rows = NI // PIECES
    pieces = [(i, j) for i in range(PIECES) for j in range(2)]

    def inward(i, j):
        at = pl.ds(i * rows, rows)
        return pltpu.make_async_copy((a, b)[j].at[at], (a_mid, b_mid)[j].at[at], in_sem.at[j, i])

    def outward(i, j):
        at = pl.ds(i * rows, rows)
        return pltpu.make_async_copy((a_mid, b_mid)[j].at[at], (a_out, b_out)[j].at[at], out_sem.at[j, i])

    for piece in pieces:
        inward(*piece).start()
    for piece in pieces:
        inward(*piece).wait()
        outward(*piece).start()
    for piece in pieces:
        outward(*piece).wait()


def body(schur, load, dscale, basis, coarse_inv, north_match, west_match):
    vmem = pl.BlockSpec(memory_space=pltpu.VMEM)
    hbm = pl.BlockSpec(memory_space=pltpu.HBM)
    dma = pltpu.SemaphoreType.DMA

    def buf(*shape, dtype=f32):
        return pltpu.VMEM(shape, dtype)

    vec = buf(NI, SC)
    half = buf(NI, SC, dtype=bf16)
    solved, left = pl.pallas_call(
        kernel,
        out_shape=[jax.ShapeDtypeStruct((NI, SC), f32)] * 2,
        in_specs=[hbm] * 7,
        out_specs=[hbm, hbm],
        scratch_shapes=[
            buf(1, NI), buf(1, F, dtype=jnp.int32), buf(1, F, dtype=jnp.int32),
            buf(NI, NI), buf(NI, NI, dtype=bf16), buf(NI, NI, dtype=bf16),
            vec, buf(2, NI, SC), vec, vec, vec, vec, half, half, buf(NI, 128),
            buf(F, F, dtype=bf16), buf(F, F, dtype=bf16), buf(16, NI), buf(4, 16, F), buf(48, NI),
            buf(96, NI, dtype=bf16), buf(96, NI, dtype=bf16), buf(NI, 256, dtype=bf16), buf(256, SC, dtype=bf16),
            buf(40, SC), buf(40, SC),
            buf(N, K, N * 128), buf(128, N * 128, dtype=bf16), buf(128, N * 128, dtype=bf16),
            buf(ROUNDS, 4, F, SC),
            buf(ROUNDS, N, 8, 128), buf(ROUNDS, N, 8, 128), buf(ROUNDS, 2, N, 1, 128), buf(ROUNDS, 2, N, 1, 128),
            buf(ROUNDS, SB, 128), buf(ROUNDS, N, SB, 128),
            buf(ROUNDS, N, 8, 128), buf(ROUNDS, N, 8, 128), buf(ROUNDS, N, 1, 128), buf(ROUNDS, 2, N, 1, 128),
            buf(128, 128, dtype=bf16),
            buf(ROUNDS, 8, 128), buf(ROUNDS, N, 8, 128), buf(ROUNDS, 8, 128), buf(ROUNDS, N, 8, 128),
            dma((7,)), dma((ROUNDS, 4)), dma((ROUNDS, 4)), dma((4,)), dma((4,)), dma((2,)), dma((2,)),
            dma((ROUNDS, 3)), dma((ROUNDS, 3)), dma((ROUNDS,)), dma((ROUNDS,)), dma((ROUNDS, 3)), dma((ROUNDS, 3)), dma((2,)),
            dma((ROUNDS,)), dma((ROUNDS,)), dma((ROUNDS,)), dma((ROUNDS,)),
        ],
        compiler_params=pltpu.CompilerParams(collective_id=0, has_side_effects=True, vmem_limit_bytes=63 << 20),
    )(
        schur.reshape(NI, NI), load.reshape(NI, SC), dscale.reshape(1, NI), basis.reshape(K, NI),
        coarse_inv, north_match.reshape(1, F), west_match.reshape(1, F),
    )
    solved, left = pl.pallas_call(
        deliver,
        out_shape=[jax.ShapeDtypeStruct((NI, SC), f32)] * 2,
        in_specs=[hbm] * 2,
        out_specs=[hbm] * 2,
        scratch_shapes=[vec, vec, dma((2, PIECES)), dma((2, PIECES))],
    )(solved, left)
    return solved.reshape(1, 1, NI, SC), left.reshape(1, 1, NI, SC)


def solution(mesh):
    placed = (
        P("row", "col", None, None),
        P("row", "col", None, None),
        P("row", "col", None),
        P("row", "col", None, None),
        P(("row", "col"), None),
        P("row", "col", None),
        P("row", "col", None),
    )
    return jax.shard_map(
        body,
        mesh=mesh,
        in_specs=placed,
        out_specs=(P("row", "col", None, None), P("row", "col", None, None)),
        check_vma=False,
    )
```

```python
import functools

import jax
import jax.numpy as jnp
from jax import lax
from jax.experimental import pallas as pl
from jax.experimental.pallas import tpu as pltpu
from jax.sharding import PartitionSpec as P

MESH = pl.DeviceIdType.MESH
F = 256
NI = 1024
SC = 256
K = 8
N = 16
SB = 16
ROUNDS = 4
CUTS = ((0, 0, 96, 96, 192, 256), (0, 96, 96, 192, 256), (0, 96, 96, 192, 256), (0, 96, 160, 208, 256))
PIECES = 4
OPP = (1, 0, 3, 2)
f32, bf16 = jnp.float32, jnp.bfloat16
NT = (((1,), (1,)), ((), ()))


def mm(a, b):
    return jnp.dot(a, b, preferred_element_type=f32)


def mm_nt(a, b):
    return lax.dot_general(a, b, NT, preferred_element_type=f32)


def split(x):
    hi = x.astype(bf16)
    return hi, (x - hi.astype(f32)).astype(bf16)


def split3(x):
    hi = x.astype(bf16)
    rest = x - hi.astype(f32)
    mid = rest.astype(bf16)
    return hi, mid, (rest - mid.astype(f32)).astype(bf16)


def kernel(
    schur_in, load_in, dscale_in, basis_in, cinv_in, north_in, west_in,
    sol_out, res_out,
    dscale, north, west,
    smat, shi, slo, y, us, r, p, s, x, uhi, ulo, dcol,
    pn, pw, bds, nbr_bds, bext, bst, gst, bcat, tcat, tau, sig,
    crow, chi, clo,
    halo, p1s, p1r, p1ns, p1nr, p2s, p2r, p3s, p3r, p3ns, p3nr, pm, d2s, d2r, d3s, d3r,
    local_sem, hs, hr, bs, br, cs, cr, s1, r1, s2, r2, s3, r3, out_sem, s4, r4, s5, r5,
):
    row, col = lax.axis_index("row"), lax.axis_index("col")
    has = (row > 0, row < N - 1, col > 0, col < N - 1)
    nbr = ((row - 1, col), (row + 1, col), (row, col - 1), (row, col + 1))
    wt = [jnp.where(h, 0.5, 1.0).astype(f32) for h in has]

    def fetch(i, src, dst):
        copy = pltpu.make_async_copy(src, dst, local_sem.at[i])
        copy.start()
        return copy

    get_small = [
        fetch(0, north_in, north), fetch(1, west_in, west), fetch(2, basis_in, bds.at[pl.ds(0, 8)]), fetch(3, dscale_in, dscale),
    ]
    get_cinv = fetch(4, cinv_in, crow.at[col])
    get_load = fetch(5, load_in, y)
    get_s = fetch(6, schur_in, smat)

    barrier = pltpu.get_barrier_semaphore()

    def greet(i, _):
        pl.semaphore_signal(barrier, inc=1, device_id=(lax.rem(row + i, N), col), device_id_type=MESH)
        for step in (0, 1, N - 1):
            other = (lax.rem(row + step, N), lax.rem(col + i, N))
            pl.semaphore_signal(barrier, inc=1, device_id=other, device_id_type=MESH)
        return 0

    lax.fori_loop(1, N, greet, 0, unroll=True)

    for copy in get_small:
        copy.wait()

    slot = lax.broadcasted_iota(jnp.int32, (F, F), 0)
    pn[...] = jnp.where(slot == north[...], 1.0, 0.0).astype(bf16)
    pw[...] = jnp.where(slot == west[...], 1.0, 0.0).astype(bf16)

    for f in range(4):

        @pl.when(jnp.logical_not(has[f]))
        def _():
            nbr_bds[f] = jnp.zeros((16, F), f32)
            for rd in range(ROUNDS):
                halo[rd, f] = jnp.zeros((F, SC), f32)
            if f < 2:
                for rd in range(ROUNDS - 1):
                    p1nr[rd, f] = jnp.zeros((N, 1, 128), f32)
                    p3nr[rd, f] = jnp.zeros((N, 1, 128), f32)

    bds[8:16] = jnp.where(lax.broadcasted_iota(jnp.int32, (8, NI), 0) == 0, dscale[...], 0.0)
    for f, perm in ((0, pn), (2, pw)):
        parts = split3(bds[:, f * F : (f + 1) * F])
        hi, mid, lo = [mm_nt(part, perm[...]) for part in parts]
        bds[:, f * F : (f + 1) * F] = (hi + mid) + lo

    pl.semaphore_wait(barrier, 4 * (N - 1))

    def when_each(fn, faces=(0, 1, 2, 3)):
        for f in faces:
            pl.when(has[f])(functools.partial(fn, f))

    def face_basis(f):
        return pltpu.make_async_remote_copy(
            src_ref=bds.at[:, pl.ds(f * F, F)], dst_ref=nbr_bds.at[OPP[f]], send_sem=bs.at[f], recv_sem=br.at[OPP[f]],
            device_id=nbr[f], device_id_type=MESH,
        )

    when_each(lambda f: face_basis(f).start())

    def copy_to(src, dst, send_sem, recv_sem, dev):
        return pltpu.make_async_remote_copy(
            src_ref=src, dst_ref=dst, send_sem=send_sem, recv_sem=recv_sem, device_id=dev, device_id_type=MESH
        )

    def along_col(first, up, src_of, dst, send_sem, recv_sem):
        def send(i, _):
            to = lax.rem(col + i, N)
            copy_to(src_of(to), dst, send_sem, recv_sem, (row - up, to)).start()
            return 0

        lax.fori_loop(first, N, send, 0, unroll=True)

    def three_rows(up_src, down_src, up_dst, down_dst, src_of, dst, send_sem, recv_sem):
        pl.when(has[0])(lambda: along_col(0, 1, lambda to: up_src.at[to], up_dst.at[col], send_sem.at[1], recv_sem.at[2]))
        pl.when(has[1])(lambda: along_col(0, -1, lambda to: down_src.at[to], down_dst.at[col], send_sem.at[2], recv_sem.at[1]))
        along_col(1, 0, src_of, dst, send_sem.at[0], recv_sem.at[0])

    def along_row(src, dst, send_sem, recv_sem):
        def send(i, _):
            copy_to(src, dst, send_sem, recv_sem, (lax.rem(row + i, N), col)).start()
            return 0

        lax.fori_loop(1, N, send, 0, unroll=True)

    def wait_many(buf, sem, count=N - 1):
        part = buf.at[pl.ds(0, count)]
        pltpu.make_async_copy(part, part, sem).wait()

    def three_waits(own, other, sem, between=None):
        wait_many(own, sem.at[0])
        if between is not None:
            between()
        for f in (0, 1):
            pl.when(has[f])(functools.partial(wait_many, other.at[f], sem.at[f + 1], N))

    get_cinv.wait()
    mine = crow.at[col]

    def send_cinv(i, _):
        copy_to(mine, mine, cs.at[0], cr.at[0], (row, lax.rem(col + 2 * i, N))).start()
        return 0

    lax.fori_loop(1, N // 2, send_cinv, 0)
    partner = col + 1 - 2 * lax.rem(col, 2)

    def pass_cinv():
        wait_many(crow, cr.at[0], N // 2 - 1)

        def send(i, _):
            block = crow.at[2 * i + lax.rem(col, 2)]
            copy_to(block, block, cs.at[1], cr.at[1], (row, partner)).start()
            return 0

        lax.fori_loop(0, N // 2, send, 0)

    def chunk(rd, q, faces=(0, 1, 2, 3)):
        cuts = CUTS[rd]
        start, rows = cuts[q], cuts[q + 1] - cuts[q]
        if rows == 0:
            return

        def one(f):
            pltpu.make_async_remote_copy(
                src_ref=y.at[pl.ds(f * F + start, rows)], dst_ref=halo.at[rd, OPP[f], pl.ds(start, rows)],
                send_sem=hs.at[rd, f], recv_sem=hr.at[rd, OPP[f]], device_id=nbr[f], device_id_type=MESH,
            ).start()

        when_each(one, faces)

    def halo_sent(rd):
        def one(f):
            part = y.at[pl.ds(f * F, F)]
            pltpu.make_async_copy(part, part, hs.at[rd, f]).wait()

        when_each(one)

    def halo_wait(rd, f):
        @pl.when(has[f])
        def _():
            part = halo.at[rd, f]
            pltpu.make_async_copy(part, part, hr.at[rd, f]).wait()

    get_load.wait()
    for f, perm in ((0, pn), (2, pw)):
        parts = split3(y[f * F : (f + 1) * F, :])
        hi, mid, lo = [mm(perm[...], part) for part in parts]
        y[f * F : (f + 1) * F, :] = (hi + mid) + lo
    vhi, vlo = split(y[...])
    uhi[...] = vhi
    ulo[...] = vlo

    chunk(0, 0)

    def wait_basis(f):
        part = nbr_bds.at[f]
        pltpu.make_async_copy(part, part, br.at[f]).wait()

    when_each(wait_basis)
    bext[...] = jnp.zeros_like(bext)
    drow = []
    for f in range(4):
        at = slice(f * F, (f + 1) * F)
        bext[0:8, at] = wt[f] * bds[0:8, at]
        bext[8 + 8 * f : 16 + 8 * f, at] = wt[f] * nbr_bds[f, 0:8]
        drow.append((wt[f] * wt[f]) * (bds[8:9, at] + nbr_bds[f, 8:9]))
    bhi, blo = split(bext[...])
    bst[0:48] = bhi
    bst[48:96] = blo

    lane = lax.broadcasted_iota(jnp.int32, (8, 128), 1)
    lane_group = lax.shift_right_logical(lane, 4)
    sub = lax.broadcasted_iota(jnp.int32, (8, 128), 0)
    lane_group16 = lax.shift_right_logical(lax.broadcasted_iota(jnp.int32, (SB, 128), 1), 4)
    diagonal = jnp.bitwise_and(lane_group - sub, 7)

    def turn(tile):
        out = tile
        for d in range(1, 8):
            out = jnp.where(diagonal == d, pltpu.roll(pltpu.roll(tile, SB * d, 1), 8 - d, 0), out)
        return out

    def to_blocks(part):
        return jnp.concatenate([turn(part[:, 0:128]), turn(part[:, 128:256])], axis=0)

    def from_blocks(part):
        return jnp.concatenate([turn(part[0:8]), turn(part[8:16])], axis=1)

    def rows_tile(rows):
        tile = jnp.zeros((8, 128), f32)
        for i, v in enumerate(rows):
            tile = jnp.where(sub == i, v, tile)
        return tile


    def contributions(rd, mat):
        both = mm(mat[...], uhi[...])
        c48 = both[0:48] + (both[48:96] + mm(mat[0:48], ulo[...]))
        own, north_part, south_part, west_part, east_part = [to_blocks(c48[8 * g : 8 * g + 8]) for g in range(5)]
        p1ns[rd, 0] = north_part.reshape(N, 1, 128)
        p1ns[rd, 1] = south_part.reshape(N, 1, 128)
        for b in range(N):
            p1s[rd, b] = rows_tile([part[b : b + 1] for part in (own, west_part, east_part)])
        p1r[rd, col] = p1s[rd, col]
        three_rows(
            p1ns.at[rd, 0], p1ns.at[rd, 1], p1nr.at[rd, 1], p1nr.at[rd, 0], lambda to: p1s.at[rd, to], p1r.at[rd, col],
            s1.at[rd], r1.at[rd],
        )

    def up_one(a):
        return jnp.concatenate([a[1:], a[:1]], axis=0)

    def down_one(a):
        return jnp.concatenate([a[N - 1 :], a[: N - 1]], axis=0)

    def gather_rows(rd, between):
        three_waits(p1r.at[rd], p1nr.at[rd], r1.at[rd], between)
        own, west_part, east_part = [
            jnp.concatenate([p1r[rd, i, g : g + 1] for i in range(N)], axis=0) for g in range(3)
        ]
        block = (own + (p1nr[rd, 0].reshape(N, 128) + p1nr[rd, 1].reshape(N, 128))) + (up_one(west_part) + down_one(east_part))
        turned = jnp.concatenate([block, jnp.zeros((128 - N, 128), f32)], axis=0).T
        rhs = turned[0:SB]
        for k in range(1, K):
            rhs = jnp.where(lane_group16 == k, pltpu.roll(turned[SB * k : SB * k + SB], SB * k, 1), rhs)
        p2s[rd] = rhs
        p2r[rd, row] = p2s[rd]
        along_row(p2s.at[rd], p2r.at[rd, row], s2.at[rd], r2.at[rd])

    def sum_tiles(buf):
        total = buf[0]
        for i in range(1, N):
            total = total + buf[i]
        return total

    def dots_row(rd, dots):
        d2s[rd] = dots
        d2r[rd, row] = dots
        along_row(d2s.at[rd], d2r.at[rd, row], s4.at[rd], r4.at[rd])

    def dots_col(rd):
        wait_many(d2r.at[rd], r4.at[rd])
        dots = sum_tiles(d2r.at[rd])
        d3s[rd] = dots
        d3r[rd, col] = dots
        along_col(1, 0, lambda to: d3s.at[rd], d3r.at[rd, col], s5.at[rd], r5.at[rd])

    def dots_total(rd):
        wait_many(d3r.at[rd], r5.at[rd])
        return sum_tiles(d3r.at[rd])

    def solve(rd):
        wait_many(p2r.at[rd], r2.at[rd])
        rhs = jnp.concatenate([p2r[rd, i] for i in range(N)], axis=1)
        hi, lo = split(rhs)
        both = mm_nt(jnp.concatenate([hi, lo], axis=0), chi[...])
        solved = both[0:SB] + (both[SB : 2 * SB] + mm_nt(hi, clo[...]))
        pieces = [solved] + [pltpu.roll(solved, 128 - SB * k, 1) for k in range(1, K)]
        own = jnp.concatenate(pieces, axis=0).T[0:N]
        east_of, west_of = up_one(own), down_one(own)
        p3ns[rd] = own.reshape(N, 1, 128)
        for i in range(N):
            p3s[rd, i] = rows_tile([part[i : i + 1] for part in (own, west_of, east_of)])
        p3r[rd, col] = p3s[rd, col]
        three_rows(
            p3ns.at[rd], p3ns.at[rd], p3nr.at[rd, 1], p3nr.at[rd, 0], lambda to: p3s.at[rd, to], p3r.at[rd, col],
            s3.at[rd], r3.at[rd],
        )

    def solutions(rd):
        three_waits(p3r.at[rd], p3nr.at[rd], r3.at[rd])
        own, west_of, east_of = [jnp.concatenate([p3r[rd, i, g : g + 1] for i in range(N)], axis=0) for g in range(3)]
        parts = [own, p3nr[rd, 0].reshape(N, 128), p3nr[rd, 1].reshape(N, 128), west_of, east_of]
        return jnp.concatenate([from_blocks(part) for part in parts], axis=0)

    def set_tau(new):
        tau[...] = new
        hi = new.astype(bf16).astype(f32)
        tcat[0:40] = hi.astype(bf16)
        tcat[64:104] = (new - hi).astype(bf16)
        tcat[128:168] = hi.astype(bf16)

    def dot_tile(delta, gamma, eps):
        tile = jnp.zeros((8, 128), f32)
        for i, v in enumerate((delta, gamma, eps)):
            if v is not None:
                tile = jnp.where(sub == 2 * i, v[:, 0:128], tile)
                tile = jnp.where(sub == 2 * i + 1, v[:, 128:256], tile)
        return tile

    def scalars(tile):
        return [jnp.concatenate([tile[2 * i : 2 * i + 1], tile[2 * i + 1 : 2 * i + 2]], axis=1) for i in range(3)]

    def prepare_rows(f):
        at = slice(f * F, (f + 1) * F)
        parts = list(split(smat[at, :]))
        for part, dst in zip(parts, (shi, slo)):
            if f == 0:
                part = mm(pn[...], part).astype(bf16)
            elif f == 2:
                part = mm(pw[...], part).astype(bf16)
            dst[at, 0:F] = mm_nt(part[:, 0:F], pn[...]).astype(bf16)
            dst[at, F : 2 * F] = part[:, F : 2 * F]
            dst[at, 2 * F : 3 * F] = mm_nt(part[:, 2 * F : 3 * F], pw[...]).astype(bf16)
            dst[at, 3 * F :] = part[:, 3 * F :]

    def new_u(rd, f):
        at = slice(f * F, (f + 1) * F)
        d = dcol[at, :]
        res = r[at, :]
        val = jnp.concatenate([d, d], axis=1) * res + mm(bcat[at, :], tcat[...])
        us[(rd + 1) % 2, at, :] = val
        hi, lo = split(val)
        uhi[at, :] = hi
        ulo[at, :] = lo
        return wt[f] * jnp.sum(res * val, axis=0, keepdims=True), val

    def own_order(f, val):
        if f in (1, 3):
            return val
        perm = (pn if f == 0 else pw)[...]
        hi, mid, lo = [
            lax.dot_general(perm, part, (((0,), (0,)), ((), ())), preferred_element_type=f32) for part in split3(val)
        ]
        return (hi + mid) + lo

    def apply_schur(rd, after_face):
        total = jnp.zeros((1, SC), f32)
        for f in range(4):
            at = slice(f * F, (f + 1) * F)
            val = mm(shi[at, :], uhi[...]) + (mm(shi[at, :], ulo[...]) + mm(slo[at, :], uhi[...]))
            y[at, :] = val
            after_face(f)
            total = total + jnp.sum(us[rd % 2, at, :] * val, axis=0, keepdims=True)
        return total

    def move(rd, alpha, beta, write):
        for f in range(4):
            at = slice(f * F, (f + 1) * F)
            direction = us[rd % 2, at, :]
            if beta is not None:
                direction = direction + beta * p[at, :]
            iterate = alpha * direction
            if beta is not None:
                iterate = iterate + x[at, :]
            if write is None:
                p[at, :] = direction
                x[at, :] = iterate
            else:
                write(f, iterate)

    contributions(0, bst)
    chunk(0, 1)
    get_s.wait()
    prepare_rows(0)
    prepare_rows(1)
    gather_rows(0, lambda: chunk(0, 2))
    pass_cinv()
    chunk(0, 3)
    prepare_rows(2)
    prepare_rows(3)
    wait_many(crow, cr.at[1], N // 2)
    order = lax.broadcasted_iota(jnp.int32, (128, 128), 0)
    order = jnp.bitwise_and(order, N - 1) * K + lax.shift_right_logical(order, 4)
    pm[...] = jnp.where(order == lax.broadcasted_iota(jnp.int32, (128, 128), 1), 1.0, 0.0).astype(bf16)
    for part, dst in zip(split(crow[...].reshape(128, N * 128)), (chi, clo)):
        part = mm(pm[...], part).astype(bf16)
        for i in range(N):
            dst[:, i * 128 : i * 128 + 128] = mm_nt(part[:, i * 128 : i * 128 + 128], pm[...]).astype(bf16)
    solve(0)
    chunk(0, 4)
    both = mm(bst[...], shi[...])
    gt = both[0:48] + (both[48:96] + mm(bst[0:48], slo[...]))
    ghi, glo = split(gt)
    gst[0:48] = ghi
    gst[48:96] = glo
    tcat[...] = jnp.zeros_like(tcat)
    bhi32 = bext[...].astype(bf16).astype(f32)
    blo32 = bext[...] - bhi32
    pad = jnp.zeros((16, NI), f32)
    bcat[...] = jnp.concatenate([bhi32, pad, bhi32, pad, blo32, pad, jnp.zeros((64, NI), f32)], axis=0).T.astype(bf16)
    dcol[...] = jnp.broadcast_to(jnp.concatenate(drow, axis=1), (128, NI)).T
    set_tau(solutions(0))
    gamma = jnp.zeros((1, SC), f32)
    for f in (3, 2, 1, 0):
        at = slice(f * F, (f + 1) * F)
        halo_wait(0, f)
        r[at, :] = y[at, :] + halo[0, f]
        gamma = gamma + new_u(0, f)[0]
    halo_sent(0)

    eps = None
    gamma_old = pap_old = pending = None
    for rd in range(1, ROUNDS):
        last = rd == ROUNDS - 1
        if not last:
            contributions(rd, gst)
        delta = apply_schur(rd, lambda f: chunk(rd, 0, (f,)))
        dots_row(rd, dot_tile(delta, gamma, eps))
        if not last:
            if pending is not None:
                move(*pending, None)
            gather_rows(rd, lambda: chunk(rd, 1))
            chunk(rd, 2)
            dots_col(rd)
            solve(rd)
            chunk(rd, 3)
            solved = solutions(rd)
        else:
            chunk(rd, 1)
            chunk(rd, 2)
            move(*pending, None)
            dots_col(rd)
            chunk(rd, 3)
        total = dots_total(rd)
        delta_t, gamma_t, eps_t = scalars(total)
        if rd == 1:
            beta = None
            pap = delta_t
        else:
            beta = gamma_t / gamma_old
            pap = delta_t + beta * (2.0 * eps_t + beta * pap_old)
        alpha = gamma_t / pap
        gamma_old, pap_old = gamma_t, pap
        if not last:
            if beta is not None:
                solved = solved + beta * sig[...]
            sig[...] = solved
            set_tau(tau[...] - alpha * solved)
        if last:

            def write(f, val):
                x[f * F : (f + 1) * F, :] = own_order(f, val)
                pltpu.make_async_copy(x.at[pl.ds(f * F, F)], sol_out.at[pl.ds(f * F, F)], out_sem.at[0]).start()

            move(rd, alpha, beta, write)
        pending = (rd, alpha, beta)
        gamma = jnp.zeros((1, SC), f32)
        eps = jnp.zeros((1, SC), f32)
        for f in (3, 2, 1, 0):
            at = slice(f * F, (f + 1) * F)
            halo_wait(rd, f)
            image = y[at, :] + halo[rd, f]
            if beta is not None:
                image = image + beta * s[at, :]
            res = r[at, :] - alpha * image
            if last:
                r[at, :] = own_order(f, res)
                pltpu.make_async_copy(r.at[pl.ds(f * F, F)], res_out.at[pl.ds(f * F, F)], out_sem.at[1]).start()
            else:
                r[at, :] = res
                s[at, :] = image
                share, val = new_u(rd, f)
                gamma = gamma + share
                eps = eps + wt[f] * jnp.sum(val * image, axis=0, keepdims=True)
        halo_sent(rd)

    pltpu.make_async_copy(x, sol_out, out_sem.at[0]).wait()
    pltpu.make_async_copy(r, res_out, out_sem.at[1]).wait()
    when_each(lambda f: face_basis(f).wait_send())
    wait_many(crow, cs.at[0], N // 2 - 1)
    wait_many(crow, cs.at[1], N // 2)
    for rd in range(ROUNDS):
        if rd < ROUNDS - 1:
            three_waits(p1r.at[rd], p1nr.at[rd], s1.at[rd])
            wait_many(p2r.at[rd], s2.at[rd])
            three_waits(p3r.at[rd], p3nr.at[rd], s3.at[rd])
        if rd > 0:
            wait_many(d2r.at[rd], s4.at[rd])
            wait_many(d3r.at[rd], s5.at[rd])


def deliver(a, b, a_out, b_out, a_mid, b_mid, in_sem, out_sem):
    rows = NI // PIECES
    pieces = [(i, j) for i in range(PIECES) for j in range(2)]

    def inward(i, j):
        at = pl.ds(i * rows, rows)
        return pltpu.make_async_copy((a, b)[j].at[at], (a_mid, b_mid)[j].at[at], in_sem.at[j, i])

    def outward(i, j):
        at = pl.ds(i * rows, rows)
        return pltpu.make_async_copy((a_mid, b_mid)[j].at[at], (a_out, b_out)[j].at[at], out_sem.at[j, i])

    for piece in pieces:
        inward(*piece).start()
    for piece in pieces:
        inward(*piece).wait()
        outward(*piece).start()
    for piece in pieces:
        outward(*piece).wait()


def body(schur, load, dscale, basis, coarse_inv, north_match, west_match):
    vmem = pl.BlockSpec(memory_space=pltpu.VMEM)
    hbm = pl.BlockSpec(memory_space=pltpu.HBM)
    dma = pltpu.SemaphoreType.DMA

    def buf(*shape, dtype=f32):
        return pltpu.VMEM(shape, dtype)

    vec = buf(NI, SC)
    half = buf(NI, SC, dtype=bf16)
    solved, left = pl.pallas_call(
        kernel,
        out_shape=[jax.ShapeDtypeStruct((NI, SC), f32)] * 2,
        in_specs=[hbm] * 7,
        out_specs=[hbm, hbm],
        scratch_shapes=[
            buf(1, NI), buf(1, F, dtype=jnp.int32), buf(1, F, dtype=jnp.int32),
            buf(NI, NI), buf(NI, NI, dtype=bf16), buf(NI, NI, dtype=bf16),
            vec, buf(2, NI, SC), vec, vec, vec, vec, half, half, buf(NI, 128),
            buf(F, F, dtype=bf16), buf(F, F, dtype=bf16), buf(16, NI), buf(4, 16, F), buf(48, NI),
            buf(96, NI, dtype=bf16), buf(96, NI, dtype=bf16), buf(NI, 256, dtype=bf16), buf(256, SC, dtype=bf16),
            buf(40, SC), buf(40, SC),
            buf(N, K, N * 128), buf(128, N * 128, dtype=bf16), buf(128, N * 128, dtype=bf16),
            buf(ROUNDS, 4, F, SC),
            buf(ROUNDS, N, 8, 128), buf(ROUNDS, N, 8, 128), buf(ROUNDS, 2, N, 1, 128), buf(ROUNDS, 2, N, 1, 128),
            buf(ROUNDS, SB, 128), buf(ROUNDS, N, SB, 128),
            buf(ROUNDS, N, 8, 128), buf(ROUNDS, N, 8, 128), buf(ROUNDS, N, 1, 128), buf(ROUNDS, 2, N, 1, 128),
            buf(128, 128, dtype=bf16),
            buf(ROUNDS, 8, 128), buf(ROUNDS, N, 8, 128), buf(ROUNDS, 8, 128), buf(ROUNDS, N, 8, 128),
            dma((7,)), dma((ROUNDS, 4)), dma((ROUNDS, 4)), dma((4,)), dma((4,)), dma((2,)), dma((2,)),
            dma((ROUNDS, 3)), dma((ROUNDS, 3)), dma((ROUNDS,)), dma((ROUNDS,)), dma((ROUNDS, 3)), dma((ROUNDS, 3)), dma((2,)),
            dma((ROUNDS,)), dma((ROUNDS,)), dma((ROUNDS,)), dma((ROUNDS,)),
        ],
        compiler_params=pltpu.CompilerParams(collective_id=0, has_side_effects=True, vmem_limit_bytes=63 << 20),
    )(
        schur.reshape(NI, NI), load.reshape(NI, SC), dscale.reshape(1, NI), basis.reshape(K, NI),
        coarse_inv, north_match.reshape(1, F), west_match.reshape(1, F),
    )
    solved, left = pl.pallas_call(
        deliver,
        out_shape=[jax.ShapeDtypeStruct((NI, SC), f32)] * 2,
        in_specs=[hbm] * 2,
        out_specs=[hbm] * 2,
        scratch_shapes=[vec, vec, dma((2, PIECES)), dma((2, PIECES))],
    )(solved, left)
    return solved.reshape(1, 1, NI, SC), left.reshape(1, 1, NI, SC)


def solution(mesh):
    placed = (
        P("row", "col", None, None),
        P("row", "col", None, None),
        P("row", "col", None),
        P("row", "col", None, None),
        P(("row", "col"), None),
        P("row", "col", None),
        P("row", "col", None),
    )
    return jax.shard_map(
        body,
        mesh=mesh,
        in_specs=placed,
        out_specs=(P("row", "col", None, None), P("row", "col", None, None)),
        check_vma=False,
    )
```
